256 devices in a mesh: gx: 32 (over x, y, core), gy: 8 (over z).
Axes of the slice: x: 4, y: 4, z: 8, core: 2. Of those that a mesh axis runs over, the one named last changes fastest.
Arguments:
- velocity: float32 [4096, 64, 1024], P('gx', None, 'gy'), may hold values from -4.5 to 4.5
- metric: float32 [4096], P('gx'), may hold values from 0.5 to 2
- lower_coupling: float32 [4096], replicated, may hold values from 1024 to 4096
- upper_coupling: float32 [4096], replicated, may hold values from 64 to 256
- cross_diffusion: float32 [1024], P('gy'), may hold values from 0.1 to 0.45
Outputs:
- derivative: float32 [4096, 64, 1024], P('gx', None, 'gy')
- updated: float32 [4096, 64, 1024], P('gx', None, 'gy')
The draws below stay inside these ranges and needn't reach their ends.
All inputs are finite; a program needn't handle non-finite values.
Results may differ from the reference program's by a relative error of at most 0.00021.
Values sent between devices are 32-bit elements; how exact they have to be, the bound alone decides.
No kernel may reach another device: no remote copies, remote signals or barrier semaphores. Data moves between devices by JAX's collectives and lax.ppermute only.
A program may use at most 128 MiB of HBM per device.

```python
import math
import jax
import jax.numpy as jnp
from jax import lax

ZW = 64
NX = 4096
NY = 1024


def draw_velocity(key, part):
    keys = jax.random.split(key, 4)
    waves = jax.random.randint(keys[0], (), 1, 4).astype(jnp.float32)
    phase = jax.random.uniform(keys[1], (), jnp.float32, -math.pi, math.pi)
    position = jnp.arange(NX).astype(jnp.float32)
    profile = 0.6 + 0.4 * jnp.sin(2.0 * math.pi * waves * position / NX + phase)
    cross = jnp.clip(jax.random.normal(keys[2], (ZW, NY), jnp.float32), -3.0, 3.0)
    noise = 0.5 * jnp.clip(jax.random.normal(keys[3], (NX, ZW, NY), jnp.float32), -3.0, 3.0)
    return profile[:, None, None] * cross[None, :, :] + noise


def shard_levels(rng, extent, cuts, low, top_value):
    def one(axis_at, shards_of):
        steps = jax.random.uniform(jax.random.fold_in(jax.random.fold_in(rng, 6), axis_at), (shards_of,), jnp.float32, low / len(cuts), top_value / len(cuts))
        return jnp.repeat(jnp.exp(steps), extent[axis_at] // shards_of).reshape((-1,) + (1,) * (len(extent) - axis_at - 1))

    level = one(*cuts[0])
    for cut in cuts[1:]:
        level = level * one(*cut)
    return level


def setup_inputs(seed: int = 0) -> dict:
    key_list = jax.random.split(jax.random.key(seed), 6)
    return {
        "velocity": draw_velocity(jax.random.fold_in(key_list[5], 71), 0),
        "metric": jnp.clip(jnp.exp(math.log(2.0) - 1.3862944 * jax.random.uniform(key_list[1], (NX,), jnp.float32) ** shard_levels(key_list[1], (NX,), ((0, 32),), -0.2, 0.2)), 0.5, 2.0),
        "lower_coupling": jnp.clip(jnp.exp(jax.random.uniform(key_list[2], (NX,), jnp.float32, math.log(1024.0), math.log(4096.0))), 1024.0, 4096.0),
        "upper_coupling": jnp.clip(jnp.exp(jax.random.uniform(key_list[3], (NX,), jnp.float32, math.log(64.0), math.log(256.0))), 64.0, 256.0),
        "cross_diffusion": jnp.clip(jnp.exp(math.log(0.45) - 1.50407736 * jax.random.uniform(key_list[4], (NY,), jnp.float32) ** shard_levels(key_list[4], (NY,), ((0, 8),), -0.2, 0.2)), 0.1, 0.45),
    }


ALPHA = 1.0 / 3.0
NEAR = 7.0 / 9.0
FAR = 1.0 / 36.0

def reference(velocity, metric, lower_coupling, upper_coupling, cross_diffusion):
    total = velocity.shape[0]
    position = jnp.arange(total)
    first = position == 0
    last = position == total - 1
    dtype = velocity.dtype
    slope_sub = jnp.where(first, jnp.zeros((total,), dtype), jnp.full((total,), ALPHA, dtype))
    slope_dia = jnp.ones((total,), dtype)
    slope_sup = jnp.where(last, jnp.zeros((total,), dtype), jnp.full((total,), ALPHA, dtype))
    viscous_sub = jnp.where(first, jnp.zeros((total,), dtype), -lower_coupling)
    viscous_dia = 1.0 + lower_coupling + upper_coupling
    viscous_sup = jnp.where(last, jnp.zeros((total,), dtype), -upper_coupling)

    def plane(field):
        rimmed = jnp.pad(field, ((2, 2), (0, 0)))
        slope_rhs = NEAR * (rimmed[3:-1] - rimmed[1:-3]) + FAR * (rimmed[4:] - rimmed[:-4])
        sides = jnp.pad(field, ((0, 0), (1, 1)))
        viscous_rhs = field + cross_diffusion[None, :] * (sides[:, 2:] - 2.0 * field + sides[:, :-2])
        slope = lax.linalg.tridiagonal_solve(slope_sub, slope_dia, slope_sup, slope_rhs)
        updated = lax.linalg.tridiagonal_solve(viscous_sub, viscous_dia, viscous_sup, viscous_rhs)
        return (metric[:, None] * slope, updated)
    derivative, updated = lax.map(plane, jnp.moveaxis(velocity, 1, 0))
    return (jnp.moveaxis(derivative, 0, 1), jnp.moveaxis(updated, 0, 1))
```

```python
import functools

import jax
import jax.numpy as jnp
import numpy as np
from jax import lax
from jax.experimental import pallas as pl
from jax.experimental.pallas import tpu as pltpu
from jax.sharding import PartitionSpec as P


ALPHA = 1.0 / 3.0
BODY = 25.0 / 36.0
DIRECT = 1.0 / 12.0
END = 1.0 / 36.0
LANES = 128
CHUNKS = 8
MIB = 1024 * 1024
F32 = jnp.float32
TOKEN = jax.ShapeDtypeStruct((8, LANES), F32)


@functools.lru_cache(maxsize=None)
def slope_constants(blocks, span):
    inner = span - 1
    off = -ALPHA
    fwd = np.ones(span)
    for i in range(1, inner):
        fwd[i] = 1.0 / (1.0 - off * off * fwd[i - 1])
    bwd = np.ones(span)
    for i in range(inner - 2, -1, -1):
        bwd[i] = 1.0 / (1.0 - off * off * bwd[i + 1])
    rho, mu, nu = (fwd.copy(), fwd * off, fwd * off)
    own = np.zeros(span + 2)
    acc = 1.0
    for i in range(inner - 1, -1, -1):
        own[i + 1] = off * rho[i] * acc
        acc *= mu[i]
    through = acc
    own[inner + 1] = 1.0
    first = np.zeros(span + 2)
    acc = 1.0
    for i in range(inner):
        first[i + 1] = bwd[i] * acc
        acc *= bwd[i] * off
    cross = acc
    own_v = np.zeros(span + 2)
    first_v = np.zeros(span + 2)
    for at in range(span + 2):
        low = own[at - 1] if at > 0 else 0.0
        high = own[at + 1] if at < span + 1 else 0.0
        own_v[at] = BODY * (low - high)
        low = first[at - 1] if at > 0 else 0.0
        high = first[at + 1] if at < span + 1 else 0.0
        first_v[at] = BODY * (low - high)
    sum_own = own_v[1 : span + 1].copy()
    sum_next = off * first_v[1 : span + 1]
    sum_next[0] += own_v[span + 1]
    low = off * through
    high = off * cross
    ends = off * bwd[0]
    red = []
    previous = 0.0
    for k in range(blocks):
        middle = 1.0 - off * nu[inner - 1] - (off * ends if k < blocks - 1 else 0.0)
        left = low if k > 0 else 0.0
        right = high if k < blocks - 1 else 0.0
        pivot = 1.0 / (middle - left * previous)
        red.append((pivot, pivot * left, pivot * right))
        previous = pivot * right
    lead = np.zeros(span)
    trail = np.ones(span)
    acc = 1.0
    for i in range(inner):
        acc *= bwd[i] * off
        lead[i] = acc
    acc = 1.0
    for i in range(inner - 1, -1, -1):
        acc *= nu[i]
        trail[i] = acc
    table = [rho * BODY, mu, nu, rho * END, sum_own, sum_next, lead, trail]
    rows = np.stack(table).astype(np.float32)
    weights = {
        "before": float(own_v[0]),
        "after": float(off * first_v[0]),
        "first_end": float(own[1] * END),
        "last_end": float(-own[inner + 1] * END),
    }
    return rows, red, weights


def lane_of(shape):
    return lax.broadcasted_iota(jnp.int32, shape, len(shape) - 1)


def vmem(mib):
    return pltpu.CompilerParams(vmem_limit_bytes=mib * MIB)


def work(ops, reads):
    return pl.CostEstimate(flops=ops, bytes_accessed=reads, transcendentals=0)


def in_vmem(count):
    return [pl.BlockSpec(memory_space=pltpu.VMEM)] * count


def in_hbm(count):
    return [pl.BlockSpec(memory_space=pltpu.HBM)] * count


def in_smem(count):
    return [pl.BlockSpec(memory_space=pltpu.SMEM)] * count


def terms_kernel(
    blocks,
    low_ref,
    up_ref,
    line_ref,
    weight_ref,
    spike_ref,
    row_ref,
    red_ref,
    kap,
    dnow,
    dpre,
    enow,
    enxt,
    factor,
    chain,
    turn,
):
    span = line_ref.shape[1]
    inner = span - 1
    index = lax.axis_index("gx")
    filler = jnp.ones((LANES - blocks, span), F32)
    lower = jnp.transpose(jnp.concatenate([low_ref[...], filler], 0))
    upper = jnp.transpose(jnp.concatenate([up_ref[...], filler], 0))
    row = lax.broadcasted_iota(jnp.int32, (span, LANES), 0)
    lane = lane_of((span, LANES))
    scale = 1.0 / (1.0 + lower + upper)
    alpha = jnp.where((row == 0) & (lane == 0), 0.0, lower * scale)
    gamma = jnp.where((row == inner) & (lane == blocks - 1), 0.0, upper * scale)
    kap[...] = alpha * pltpu.roll(gamma, 1, 0)
    one = jnp.ones((1, LANES), F32)
    dnow[0:1, :] = one
    dpre[0:1, :] = one
    enow[inner - 1 : inner, :] = one
    enxt[inner - 1 : inner, :] = one
    for ref in (dnow, dpre, enow, enxt):
        ref[inner:span, :] = one
    d1, d2, e1, e2 = (one, one, one, one)
    for i in range(1, inner):
        d0 = d1 - kap[i : i + 1, :] * d2
        dpre[i : i + 1, :] = d1
        dnow[i : i + 1, :] = d0
        d2, d1 = (d1, d0)
        j = inner - 1 - i
        e0 = e1 - kap[j + 1 : j + 2, :] * e2
        enxt[j : j + 1, :] = e1
        enow[j : j + 1, :] = e0
        e2, e1 = (e1, e0)
    fwd = dpre[...] / dnow[...]
    bwd = enxt[...] / enow[...]
    rho, mu, nu = (fwd * scale, fwd * alpha, fwd * gamma)
    factor[0] = mu
    factor[1] = bwd * gamma
    factor[2] = bwd * alpha
    factor[3] = nu
    h_acc, g_acc, l_acc, t_acc = (one, one, one, one)
    for i in range(inner):
        j = inner - 1 - i
        chain[0, j : j + 1, :] = h_acc
        chain[1, i : i + 1, :] = g_acc
        h_acc = h_acc * factor[0, j : j + 1, :]
        g_acc = g_acc * factor[1, i : i + 1, :]
        l_acc = l_acc * factor[2, i : i + 1, :]
        t_acc = t_acc * factor[3, j : j + 1, :]
        chain[2, i : i + 1, :] = l_acc
        chain[3, j : j + 1, :] = t_acc
    zero = jnp.zeros((1, LANES), F32)
    chain[0, inner:span, :] = one
    chain[1, inner:span, :] = zero
    chain[2, inner:span, :] = zero
    chain[3, inner:span, :] = one
    alpha_end = alpha[inner:span, :]
    gamma_end = gamma[inner:span, :]
    own = jnp.where(row == inner, 1.0, alpha_end * chain[0]) * rho
    first = bwd * scale * chain[1] * pltpu.roll(gamma_end, 1, 1)
    inflow = bwd[0:1, :] * alpha[0:1, :]
    middle = (
        1.0
        - alpha_end * nu[inner - 1 : inner, :]
        - gamma_end * pltpu.roll(inflow, LANES - 1, 1)
    )
    scale_red = 1.0 / middle
    left = alpha_end * h_acc * scale_red
    right = gamma_end * pltpu.roll(t_acc, LANES - 1, 1) * scale_red
    product = left * pltpu.roll(right, 1, 1)
    for at, value in enumerate((scale_red, left, right, product)):
        turn[at] = jnp.transpose(jnp.broadcast_to(value, (LANES, LANES)))
    d1, d2 = (one, one)
    for k in range(blocks):
        if k == 0:
            ratio = one
        else:
            d0 = d1 - turn[3, k : k + 1, :] * d2
            ratio = d1 / d0
            d2, d1 = (d1, d0)
        for at in range(3):
            red_ref[at, k : k + 1, :] = turn[at, k : k + 1, :] * ratio

    def mine(value):
        column = jnp.sum(jnp.where(lane == index, value, 0.0), axis=1, keepdims=True)
        return jnp.broadcast_to(column, (span, LANES))

    line_ref[0] = mine(rho)
    line_ref[1] = mine(mu)
    line_ref[2] = mine(nu)
    spike_ref[0] = mine(chain[2])
    spike_ref[1] = mine(chain[3])
    for at, value in enumerate((own, first)):
        here = mine(value)
        weight_ref[at] = here
        row_ref[at] = jnp.transpose(here)[0:8, :]


def viscous_terms(lower, upper):
    blocks, span = lower.shape
    square = pltpu.VMEM((span, LANES), F32)
    four = pltpu.VMEM((4, span, LANES), F32)
    return pl.pallas_call(
        functools.partial(terms_kernel, blocks),
        out_shape=(
            jax.ShapeDtypeStruct((3, span, LANES), F32),
            jax.ShapeDtypeStruct((2, span, LANES), F32),
            jax.ShapeDtypeStruct((2, span, LANES), F32),
            jax.ShapeDtypeStruct((2, 8, span), F32),
            jax.ShapeDtypeStruct((3, blocks, LANES), F32),
        ),
        in_specs=in_vmem(2),
        out_specs=tuple(in_vmem(5)),
        scratch_shapes=[square] * 5 + [four, four, pltpu.VMEM((4, LANES, LANES), F32)],
        compiler_params=vmem(8),
        cost_estimate=work(4 * 1024 * 1024, 1024 * 1024),
        name="viscous_terms",
    )(lower, upper)


def chunk_copy(source, target, sem, c):
    rows = source.shape[0] // CHUNKS
    where = pl.ds(c * rows, rows)
    return pltpu.make_async_copy(source.at[where], target.at[where], sem.at[c])


def start_all(source, target, sem):
    for c in range(CHUNKS):
        chunk_copy(source, target, sem, c).start()


def streamed(shape, count):
    return [pltpu.VMEM(shape, F32)] * count


def rim_kernel(v_hbm, first_ref, last_ref, v_buf, sem):
    span, planes, width = v_buf.shape
    rows = span // CHUNKS
    start_all(v_hbm, v_buf, sem)
    lane = lane_of((planes, width))
    zero = jnp.zeros((planes, width), F32)

    def step(c, carry):
        first, last = carry
        chunk_copy(v_hbm, v_buf, sem, c).wait()
        for r in range(rows):
            i = c * rows + r
            turned = pltpu.roll(v_buf[i], i, 1)
            first = jnp.where(lane == i, turned, first)
            last = jnp.where(lane == lax.rem(i + width - 1, width), turned, last)
        return (first, last)

    first, last = lax.fori_loop(0, CHUNKS, step, (zero, zero))
    first_ref[...] = first
    last_ref[...] = pltpu.roll(last, 1, 1)


def rim_columns(velocity):
    span, planes, width = velocity.shape
    column = jax.ShapeDtypeStruct((planes, width), F32)
    return pl.pallas_call(
        rim_kernel,
        out_shape=(column, column),
        in_specs=in_hbm(1),
        out_specs=tuple(in_vmem(2)),
        scratch_shapes=streamed(velocity.shape, 1) + [pltpu.SemaphoreType.DMA((CHUNKS,))],
        compiler_params=vmem(8),
        name="rim_columns",
    )(velocity)


def sums_kernel(table, v_hbm, weight, vec_ref, v_buf, sem):
    span, planes, width = v_buf.shape
    rows = span // CHUNKS
    start_all(v_hbm, v_buf, sem)
    zero = jnp.zeros((planes, width), F32)

    def step(c, carry):
        a, b, s, t = carry
        chunk_copy(v_hbm, v_buf, sem, c).wait()
        for r in range(rows):
            i = c * rows + r
            v = v_buf[i]
            a = a + weight[0, pl.ds(i, 1), :] * v
            b = b + weight[1, pl.ds(i, 1), :] * v
            s = s + table[4, i] * v
            t = t + table[5, i] * v
        return (a, b, s, t)

    sums = lax.fori_loop(0, CHUNKS, step, (zero, zero, zero, zero))
    for at in range(4):
        vec_ref[at] = sums[at]
    vec_ref[4] = v_buf[0]
    vec_ref[5] = v_buf[span - 1]


def local_sums(table, velocity, weight):
    span, planes, width = velocity.shape
    return pl.pallas_call(
        sums_kernel,
        out_shape=jax.ShapeDtypeStruct((6, planes, width), F32),
        in_specs=in_smem(1) + in_hbm(1) + in_vmem(1),
        out_specs=in_vmem(1)[0],
        scratch_shapes=streamed(velocity.shape, 1) + [pltpu.SemaphoreType.DMA((CHUNKS,))],
        compiler_params=vmem(8),
        cost_estimate=work(8 * velocity.size, 4 * velocity.size),
        name="local_sums",
    )(table, velocity, weight)


def slope_kernel(table, metric, v_hbm, order, out_hbm, v_ref, der, v_sem, out_sem):
    span, planes, width = v_ref.shape
    inner = span - 1
    rows = span // CHUNKS
    start_all(v_hbm, v_ref, v_sem)
    zero = jnp.zeros((planes, width), F32)
    top = jnp.where(lax.axis_index("gx") == 0, 1.0, 0.0).astype(F32)

    def forward(i, carry):
        v_low, v, slo = carry
        v_high = v_ref[i + 1]
        slo = table[0, i] * (v_high - v_low) + table[1, i] * slo
        if isinstance(i, int) and i == 0:
            slo = slo + (table[3, 0] * top) * v
        der[i] = slo
        return (v, v_high, slo)

    def down(c, carry):
        chunk_copy(v_hbm, v_ref, v_sem, c + 1).wait()
        for r in range(rows):
            carry = forward(c * rows + r, carry)
        return carry

    chunk_copy(v_hbm, v_ref, v_sem, 0).wait()
    carry = down(0, (zero, v_ref[0], zero))
    carry = lax.fori_loop(1, CHUNKS - 1, down, carry)
    for i in range(span - rows, inner):
        carry = forward(i, carry)

    def finish(i, slo, difference):
        scale = metric[i]
        return scale * slo + (scale * DIRECT) * difference

    def backward(i, slo, difference):
        slo = der[i] + table[2, i] * slo
        der[i] = finish(i, slo, difference)
        return slo

    def up(step, slo):
        c = CHUNKS - 1 - step
        for r in range(rows - 1, -1, -1):
            i = c * rows + r
            slo = backward(i, slo, v_ref[i + 1] - v_ref[i - 1])
        chunk_copy(der, out_hbm, out_sem, c).start()
        return slo

    der[inner] = finish(inner, zero, -v_ref[inner - 1])
    slo = zero
    for i in range(inner - 1, span - 1 - rows, -1):
        slo = backward(i, slo, v_ref[i + 1] - v_ref[i - 1])
    chunk_copy(der, out_hbm, out_sem, CHUNKS - 1).start()
    slo = lax.fori_loop(1, CHUNKS - 1, up, slo)
    for i in range(rows - 1, -1, -1):
        slo = backward(i, slo, v_ref[i + 1] - v_ref[i - 1] if i else v_ref[1])
    chunk_copy(der, out_hbm, out_sem, 0).start()
    for c in range(CHUNKS):
        chunk_copy(der, out_hbm, out_sem, c).wait()


def slope_solve(table, metric, velocity, order):
    return pl.pallas_call(
        slope_kernel,
        out_shape=pltpu.HBM(velocity.shape, F32),
        in_specs=in_smem(2) + in_hbm(1) + [pl.BlockSpec(memory_space=pl.ANY)],
        out_specs=in_hbm(1)[0],
        scratch_shapes=streamed(velocity.shape, 2) + [pltpu.SemaphoreType.DMA((CHUNKS,))] * 2,
        compiler_params=vmem(12),
        cost_estimate=work(12 * velocity.size, 12 * velocity.size),
        name="slope_solve",
    )(table, metric, velocity, order)


def viscous_kernel(
    v_hbm,
    line,
    before_ref,
    after_ref,
    cross_ref,
    order,
    out_hbm,
    v_ref,
    upd,
    even,
    odd,
    v_sem,
    out_sem,
):
    span, planes, width = v_ref.shape
    inner = span - 1
    rows = span // CHUNKS
    start_all(v_hbm, v_ref, v_sem)
    lane = lane_of((planes, width))
    ahead = pltpu.roll(after_ref[...], width - 1, 1)
    even[...] = jnp.where(lax.rem(lane, 2) == 0, before_ref[...], ahead)
    odd[...] = jnp.where(lax.rem(lane, 2) == 1, before_ref[...], ahead)
    cross = jnp.broadcast_to(cross_ref[...], (planes, width))
    keep = 1.0 - 2.0 * cross
    zero = jnp.zeros((planes, width), F32)

    def forward(i, r, vis):
        v = v_ref[i]
        rim = pltpu.roll((odd if r % 2 else even)[...], lax.rem(width - i, width), 1)
        low = jnp.where(lane == 0, rim, pltpu.roll(v, 1, 1))
        high = jnp.where(lane == width - 1, rim, pltpu.roll(v, width - 1, 1))
        rhs = keep * v + cross * (low + high)
        vis = line[0, pl.ds(i, 1), :] * rhs + line[1, pl.ds(i, 1), :] * vis
        upd[i] = vis
        return vis

    def down(c, vis):
        chunk_copy(v_hbm, v_ref, v_sem, c).wait()
        for r in range(rows):
            vis = forward(c * rows + r, r, vis)
        return vis

    lax.fori_loop(0, CHUNKS, down, zero)

    def backward(i, vis):
        vis = upd[i] + line[2, pl.ds(i, 1), :] * vis
        upd[i] = vis
        return vis

    def up(step, vis):
        c = CHUNKS - 1 - step
        for r in range(rows - 1, -1, -1):
            vis = backward(c * rows + r, vis)
        chunk_copy(upd, out_hbm, out_sem, c).start()
        return vis

    upd[inner] = zero
    vis = zero
    for i in range(inner - 1, span - 1 - rows, -1):
        vis = backward(i, vis)
    chunk_copy(upd, out_hbm, out_sem, CHUNKS - 1).start()
    lax.fori_loop(1, CHUNKS, up, vis)
    for c in range(CHUNKS):
        chunk_copy(upd, out_hbm, out_sem, c).wait()


def viscous_solve(velocity, line, before, after, cross, order):
    span, planes, width = velocity.shape
    return pl.pallas_call(
        viscous_kernel,
        out_shape=pltpu.HBM(velocity.shape, F32),
        in_specs=in_hbm(1) + in_vmem(4) + [pl.BlockSpec(memory_space=pl.ANY)],
        out_specs=in_hbm(1)[0],
        scratch_shapes=streamed(velocity.shape, 2)
        + [pltpu.VMEM((planes, width), F32)] * 2
        + [pltpu.SemaphoreType.DMA((CHUNKS,))] * 2,
        compiler_params=vmem(12),
        cost_estimate=work(12 * velocity.size, 12 * velocity.size),
        name="viscous_solve",
    )(velocity, line, before, after, cross, order)


def wall_normal(value, before, after, cross):
    shape = value.shape
    lane = lane_of(shape)
    low = jnp.where(lane == 0, before, pltpu.roll(value, 1, 1))
    high = jnp.where(lane == shape[1] - 1, after, pltpu.roll(value, shape[1] - 1, 1))
    return (1.0 - 2.0 * cross) * value + cross * (low + high)


def pack_kernel(vec_ref, row_ref, before_ref, after_ref, cross_ref, out_ref, token):
    blocks = out_ref.shape[0]
    part = vec_ref.shape[1] // blocks
    cross = cross_ref[...]
    vectors = []
    for at in range(2):
        weights = row_ref[at, 0:1, :]
        before = jnp.sum(before_ref[...] * weights, axis=1, keepdims=True)
        after = jnp.sum(after_ref[...] * weights, axis=1, keepdims=True)
        vectors.append(wall_normal(vec_ref[at], before, after, cross))
    vectors += [vec_ref[at] for at in range(2, 6)]
    for at, value in enumerate(vectors):
        for m in range(blocks):
            out_ref[m, part * at : part * (at + 1), :] = value[part * m : part * (m + 1), :]
    rest = out_ref.shape[1] - 6 * part
    if rest:
        out_ref[:, 6 * part :, :] = jnp.zeros((blocks, rest, out_ref.shape[2]), F32)
    token[...] = jnp.zeros(token.shape, F32)


def rows_sent(part):
    return -(-6 * part // 8) * 8


def pack(vec, row, before, after, cross, blocks):
    _, planes, width = vec.shape
    part = planes // blocks
    return pl.pallas_call(
        pack_kernel,
        out_shape=(jax.ShapeDtypeStruct((blocks, rows_sent(part), width), F32), TOKEN),
        compiler_params=vmem(8),
        name="pack_sums",
    )(vec, row, before, after, cross)


def reduced_kernel(part, red, weights, coef_ref, in_ref, order, out_ref, token):
    blocks, rows, width = in_ref.shape
    slope_after, slope_before = (weights["after"], weights["before"])

    def piece(k, at):
        return in_ref[k, part * at : part * (at + 1), :]

    zero = jnp.zeros((part, width), F32)
    vis, slo = (zero, zero)
    vis_all, slo_all = ([], [])
    for k in range(blocks):
        vis_rhs = piece(k, 0)
        slo_rhs = piece(k, 2)
        if k < blocks - 1:
            vis_rhs = vis_rhs + piece(k + 1, 1)
            slo_rhs = slo_rhs + piece(k + 1, 3) + slope_after * piece(k, 5)
        else:
            slo_rhs = slo_rhs + weights["last_end"] * piece(k, 5)
        if k > 0:
            slo_rhs = slo_rhs + slope_before * piece(k - 1, 5)
        else:
            slo_rhs = slo_rhs + weights["first_end"] * piece(k, 4)
        vis = coef_ref[0, k : k + 1, :] * vis_rhs + coef_ref[1, k : k + 1, :] * vis
        slo = red[k][0] * slo_rhs + red[k][1] * slo
        vis_all.append(vis)
        slo_all.append(slo)
    vis, slo = (zero, zero)
    rest = rows - 6 * part
    for k in range(blocks - 1, -1, -1):
        vis = vis_all[k] + coef_ref[2, k : k + 1, :] * vis
        slo = slo_all[k] + red[k][2] * slo
        out_ref[k, part : 2 * part, :] = vis
        out_ref[k, 3 * part : 4 * part, :] = slo
        if k < blocks - 1:
            out_ref[k + 1, 0:part, :] = vis
            out_ref[k + 1, 2 * part : 3 * part, :] = slo + (BODY / ALPHA) * piece(k, 5)
        else:
            out_ref[0, 0:part, :] = zero
            out_ref[0, 2 * part : 3 * part, :] = zero
        out_ref[k, 4 * part : 5 * part, :] = piece(k - 1, 5) if k > 0 else zero
        out_ref[k, 5 * part : 6 * part, :] = piece(k + 1, 4) if k < blocks - 1 else zero
    if rest:
        out_ref[:, 6 * part :, :] = jnp.zeros((blocks, rest, width), F32)
    token[...] = jnp.zeros(token.shape, F32)


def reduced_solve(coef, arrived, order, red, weights, part):
    return pl.pallas_call(
        functools.partial(reduced_kernel, part, red, weights),
        out_shape=(jax.ShapeDtypeStruct(arrived.shape, F32), TOKEN),
        in_specs=in_vmem(2) + in_hbm(1),
        out_specs=tuple(in_vmem(2)),
        compiler_params=vmem(8),
        name="reduced_solve",
    )(coef, arrived, order)


def final_kernel(
    table,
    metric,
    der_in,
    upd_in,
    edge_ref,
    spike,
    der_hbm,
    upd_hbm,
    der,
    upd,
    edges,
    der_from,
    upd_from,
    der_to,
    upd_to,
):
    span, planes, width = der.shape
    blocks = edge_ref.shape[0]
    part = planes // blocks
    rows = span // CHUNKS
    for c in range(CHUNKS):
        chunk_copy(der_in, der, der_from, c).start()
        chunk_copy(upd_in, upd, upd_from, c).start()
    for at in range(6):
        for m in range(blocks):
            edges[at, part * m : part * (m + 1), :] = edge_ref[m, part * at : part * (at + 1), :]
    vis_low, vis_high, slo_low, slo_high = (edges[at] for at in range(4))

    def step(c, carry):
        chunk_copy(der_in, der, der_from, c).wait()
        chunk_copy(upd_in, upd, upd_from, c).wait()
        for r in range(rows):
            i = c * rows + r
            scale = metric[i]
            der[i] = der[i] + (scale * table[6, i]) * slo_low + (scale * table[7, i]) * slo_high
            upd[i] = (
                upd[i] + spike[0, pl.ds(i, 1), :] * vis_low + spike[1, pl.ds(i, 1), :] * vis_high
            )
        if isinstance(c, int) and c == 0:
            der[0] = der[0] - (metric[0] * DIRECT) * edges[4]
        if isinstance(c, int) and c == CHUNKS - 1:
            der[span - 1] = der[span - 1] + (metric[span - 1] * DIRECT) * edges[5]
        chunk_copy(der, der_hbm, der_to, c).start(priority=1)
        chunk_copy(upd, upd_hbm, upd_to, c).start(priority=1)
        return carry

    step(0, 0)
    lax.fori_loop(1, CHUNKS - 1, step, 0)
    step(CHUNKS - 1, 0)
    for c in range(CHUNKS):
        chunk_copy(der, der_hbm, der_to, c).wait()
        chunk_copy(upd, upd_hbm, upd_to, c).wait()


def final_solve(table, metric, der, upd, edge, spike):
    span, planes, width = der.shape
    result = jax.ShapeDtypeStruct(der.shape, F32)
    return pl.pallas_call(
        final_kernel,
        out_shape=(result, result),
        in_specs=in_smem(2) + in_hbm(2) + in_vmem(2),
        out_specs=tuple(in_hbm(2)),
        scratch_shapes=streamed(der.shape, 2)
        + [pltpu.VMEM((6, planes, width), F32)]
        + [pltpu.SemaphoreType.DMA((CHUNKS,))] * 4,
        compiler_params=vmem(16),
        name="final_solve",
    )(table, metric, der, upd, edge, spike)


def body(velocity, metric, lower_coupling, upper_coupling, cross_diffusion):
    span, planes, width = velocity.shape
    blocks = lax.axis_size("gx")
    walls = lax.axis_size("gy")
    part = planes // blocks
    rows, red, weights = slope_constants(blocks, span)
    table = jnp.asarray(rows)
    cross = cross_diffusion.reshape(1, width)
    line, weight, spike, row, coef = viscous_terms(
        lower_coupling.reshape(blocks, span), upper_coupling.reshape(blocks, span)
    )
    field = pltpu.with_memory_space_constraint(velocity, pltpu.HBM)
    first, last = rim_columns(field)
    up = [(j, j + 1) for j in range(walls - 1)]
    down = [(j + 1, j) for j in range(walls - 1)]
    before = lax.ppermute(last, "gy", up)
    after = lax.ppermute(first, "gy", down)
    vec = local_sums(table, field, weight)
    packed, token = pack(vec, row, before, after, cross, blocks)
    arrived = lax.all_to_all(packed, "gx", 0, 0, tiled=True)
    der = slope_solve(table, metric, field, token)
    der = pltpu.with_memory_space_constraint(der, pltpu.HBM)
    solved, token = reduced_solve(coef, arrived, der, red, weights, part)
    edge = lax.all_to_all(solved, "gx", 0, 0, tiled=True)
    upd = viscous_solve(field, line, before, after, cross, token)
    upd = pltpu.with_memory_space_constraint(upd, pltpu.HBM)
    return final_solve(table, metric, der, upd, edge, spike)


def solution(mesh):
    return jax.shard_map(
        body,
        mesh=mesh,
        in_specs=(P("gx", None, "gy"), P("gx"), P(), P(), P("gy")),
        out_specs=(P("gx", None, "gy"), P("gx", None, "gy")),
        check_vma=False,
    )
```

```python
import functools

import jax
import jax.numpy as jnp
import numpy as np
from jax import lax
from jax.experimental import pallas as pl
from jax.experimental.pallas import tpu as pltpu
from jax.sharding import PartitionSpec as P


ALPHA = 1.0 / 3.0
BODY = 25.0 / 36.0
DIRECT = 1.0 / 12.0
END = 1.0 / 36.0
LANES = 128
CHUNKS = 8
KEPT = 5
MIB = 1024 * 1024
F32 = jnp.float32
TOKEN = jax.ShapeDtypeStruct((8, LANES), F32)


@functools.lru_cache(maxsize=None)
def slope_constants(blocks, span):
    inner = span - 1
    off = -ALPHA
    fwd = np.ones(span)
    for i in range(1, inner):
        fwd[i] = 1.0 / (1.0 - off * off * fwd[i - 1])
    bwd = np.ones(span)
    for i in range(inner - 2, -1, -1):
        bwd[i] = 1.0 / (1.0 - off * off * bwd[i + 1])
    rho, mu, nu = (fwd.copy(), fwd * off, fwd * off)
    own = np.zeros(span + 2)
    acc = 1.0
    for i in range(inner - 1, -1, -1):
        own[i + 1] = off * rho[i] * acc
        acc *= mu[i]
    through = acc
    own[inner + 1] = 1.0
    first = np.zeros(span + 2)
    acc = 1.0
    for i in range(inner):
        first[i + 1] = bwd[i] * acc
        acc *= bwd[i] * off
    cross = acc
    own_v = np.zeros(span + 2)
    first_v = np.zeros(span + 2)
    for at in range(span + 2):
        low = own[at - 1] if at > 0 else 0.0
        high = own[at + 1] if at < span + 1 else 0.0
        own_v[at] = BODY * (low - high)
        low = first[at - 1] if at > 0 else 0.0
        high = first[at + 1] if at < span + 1 else 0.0
        first_v[at] = BODY * (low - high)
    sum_own = own_v[1 : span + 1].copy()
    sum_next = off * first_v[1 : span + 1]
    sum_next[0] += own_v[span + 1]
    low = off * through
    high = off * cross
    ends = off * bwd[0]
    red = []
    previous = 0.0
    for k in range(blocks):
        middle = 1.0 - off * nu[inner - 1] - (off * ends if k < blocks - 1 else 0.0)
        left = low if k > 0 else 0.0
        right = high if k < blocks - 1 else 0.0
        pivot = 1.0 / (middle - left * previous)
        red.append((pivot, pivot * left, pivot * right))
        previous = pivot * right
    lead = np.zeros(span)
    trail = np.ones(span)
    acc = 1.0
    for i in range(inner):
        acc *= bwd[i] * off
        lead[i] = acc
    acc = 1.0
    for i in range(inner - 1, -1, -1):
        acc *= nu[i]
        trail[i] = acc
    table = [rho * BODY, mu, nu, rho * END, sum_own, sum_next, lead, trail]
    rows = np.stack(table).astype(np.float32)
    weights = {
        "before": float(own_v[0]),
        "after": float(off * first_v[0]),
        "first_end": float(own[1] * END),
        "last_end": float(-own[inner + 1] * END),
    }
    return rows, red, weights


def lane_of(shape):
    return lax.broadcasted_iota(jnp.int32, shape, len(shape) - 1)


def vmem(mib):
    return pltpu.CompilerParams(vmem_limit_bytes=mib * MIB)


def work(ops, reads):
    return pl.CostEstimate(flops=ops, bytes_accessed=reads, transcendentals=0)


def in_vmem(count):
    return [pl.BlockSpec(memory_space=pltpu.VMEM)] * count


def in_hbm(count):
    return [pl.BlockSpec(memory_space=pltpu.HBM)] * count


def in_smem(count):
    return [pl.BlockSpec(memory_space=pltpu.SMEM)] * count


def viscous_terms(
    blocks,
    low_ref,
    up_ref,
    line_ref,
    weight_ref,
    spike_ref,
    row_ref,
    red_ref,
    kap,
    dnow,
    dpre,
    enow,
    enxt,
    factor,
    chain,
    turn,
):
    span = line_ref.shape[1]
    inner = span - 1
    index = lax.axis_index("gx")
    filler = jnp.ones((LANES - blocks, span), F32)
    lower = jnp.transpose(jnp.concatenate([low_ref[...], filler], 0))
    upper = jnp.transpose(jnp.concatenate([up_ref[...], filler], 0))
    row = lax.broadcasted_iota(jnp.int32, (span, LANES), 0)
    lane = lane_of((span, LANES))
    scale = 1.0 / (1.0 + lower + upper)
    alpha = jnp.where((row == 0) & (lane == 0), 0.0, lower * scale)
    gamma = jnp.where((row == inner) & (lane == blocks - 1), 0.0, upper * scale)
    kap[...] = alpha * pltpu.roll(gamma, 1, 0)
    one = jnp.ones((1, LANES), F32)
    dnow[0:1, :] = one
    dpre[0:1, :] = one
    enow[inner - 1 : inner, :] = one
    enxt[inner - 1 : inner, :] = one
    for ref in (dnow, dpre, enow, enxt):
        ref[inner:span, :] = one
    d1, d2, e1, e2 = (one, one, one, one)
    for i in range(1, inner):
        d0 = d1 - kap[i : i + 1, :] * d2
        dpre[i : i + 1, :] = d1
        dnow[i : i + 1, :] = d0
        d2, d1 = (d1, d0)
        j = inner - 1 - i
        e0 = e1 - kap[j + 1 : j + 2, :] * e2
        enxt[j : j + 1, :] = e1
        enow[j : j + 1, :] = e0
        e2, e1 = (e1, e0)
    fwd = dpre[...] / dnow[...]
    bwd = enxt[...] / enow[...]
    rho, mu, nu = (fwd * scale, fwd * alpha, fwd * gamma)
    factor[0] = mu
    factor[1] = bwd * gamma
    factor[2] = bwd * alpha
    factor[3] = nu
    h_acc, g_acc, l_acc, t_acc = (one, one, one, one)
    for i in range(inner):
        j = inner - 1 - i
        chain[0, j : j + 1, :] = h_acc
        chain[1, i : i + 1, :] = g_acc
        h_acc = h_acc * factor[0, j : j + 1, :]
        g_acc = g_acc * factor[1, i : i + 1, :]
        l_acc = l_acc * factor[2, i : i + 1, :]
        t_acc = t_acc * factor[3, j : j + 1, :]
        chain[2, i : i + 1, :] = l_acc
        chain[3, j : j + 1, :] = t_acc
    zero = jnp.zeros((1, LANES), F32)
    chain[0, inner:span, :] = one
    chain[1, inner:span, :] = zero
    chain[2, inner:span, :] = zero
    chain[3, inner:span, :] = one
    alpha_end = alpha[inner:span, :]
    gamma_end = gamma[inner:span, :]
    own = jnp.where(row == inner, 1.0, alpha_end * chain[0]) * rho
    first = bwd * scale * chain[1] * pltpu.roll(gamma_end, 1, 1)
    inflow = bwd[0:1, :] * alpha[0:1, :]
    middle = (
        1.0
        - alpha_end * nu[inner - 1 : inner, :]
        - gamma_end * pltpu.roll(inflow, LANES - 1, 1)
    )
    scale_red = 1.0 / middle
    left = alpha_end * h_acc * scale_red
    right = gamma_end * pltpu.roll(t_acc, LANES - 1, 1) * scale_red
    product = left * pltpu.roll(right, 1, 1)
    for at, value in enumerate((scale_red, left, right, product)):
        turn[at] = jnp.transpose(jnp.broadcast_to(value, (LANES, LANES)))
    d1, d2 = (one, one)
    for k in range(blocks):
        if k == 0:
            ratio = one
        else:
            d0 = d1 - turn[3, k : k + 1, :] * d2
            ratio = d1 / d0
            d2, d1 = (d1, d0)
        for at in range(3):
            red_ref[at, k : k + 1, :] = turn[at, k : k + 1, :] * ratio

    def mine(value):
        column = jnp.sum(jnp.where(lane == index, value, 0.0), axis=1, keepdims=True)
        return jnp.broadcast_to(column, (span, LANES))

    line_ref[0] = mine(rho)
    line_ref[1] = mine(mu)
    line_ref[2] = mine(nu)
    spike_ref[0] = mine(chain[2])
    spike_ref[1] = mine(chain[3])
    for at, value in enumerate((own, first)):
        here = mine(value)
        weight_ref[at] = here
        row_ref[at] = jnp.transpose(here)[0:8, :]


def chunk_copy(source, target, sem, c):
    rows = source.shape[0] // CHUNKS
    where = pl.ds(c * rows, rows)
    return pltpu.make_async_copy(source.at[where], target.at[where], sem.at[c])


def row_copy(source, target, sem, c, rows):
    where = pl.ds(c * rows, rows)
    return pltpu.make_async_copy(source.at[where], target.at[where], sem.at[c])


def start_all(source, target, sem):
    for c in range(CHUNKS):
        chunk_copy(source, target, sem, c).start()


def streamed(shape, count):
    return [pltpu.VMEM(shape, F32)] * count


def block_terms(lower, upper):
    blocks, span = lower.shape
    square = pltpu.VMEM((span, LANES), F32)
    four = pltpu.VMEM((4, span, LANES), F32)
    return pl.pallas_call(
        functools.partial(viscous_terms, blocks),
        out_shape=(
            jax.ShapeDtypeStruct((3, span, LANES), F32),
            jax.ShapeDtypeStruct((2, span, LANES), F32),
            jax.ShapeDtypeStruct((2, span, LANES), F32),
            jax.ShapeDtypeStruct((2, 8, span), F32),
            jax.ShapeDtypeStruct((3, blocks, LANES), F32),
        ),
        in_specs=in_vmem(2),
        out_specs=tuple(in_vmem(5)),
        scratch_shapes=[square] * 5
        + [four, four, pltpu.VMEM((4, LANES, LANES), F32)],
        compiler_params=vmem(8),
        cost_estimate=work(4 * MIB, MIB),
        name="block_terms",
    )(lower, upper)


def rim_kernel(v_hbm, v_ref, first_ref, last_ref, v_sem):
    span, planes, width = v_ref.shape
    rows = span // CHUNKS
    start_all(v_hbm, v_ref, v_sem)
    lane = lane_of((planes, width))
    zero = jnp.zeros((planes, width), F32)

    def step(c, carry):
        first, last = carry
        chunk_copy(v_hbm, v_ref, v_sem, c).wait()
        for r in range(rows):
            i = c * rows + r
            turned = pltpu.roll(v_ref[i], i, 1)
            first = jnp.where(lane == i, turned, first)
            last = jnp.where(lane == lax.rem(i + width - 1, width), turned, last)
        return (first, last)

    first, last = lax.fori_loop(0, CHUNKS, step, (zero, zero))
    first_ref[...] = first
    last_ref[...] = pltpu.roll(last, 1, 1)


def rim_columns(velocity):
    span, planes, width = velocity.shape
    column = jax.ShapeDtypeStruct((planes, width), F32)
    return pl.pallas_call(
        rim_kernel,
        out_shape=(pltpu.VMEM(velocity.shape, F32), column, column),
        in_specs=in_hbm(1),
        out_specs=tuple(in_vmem(3)),
        scratch_shapes=[pltpu.SemaphoreType.DMA((CHUNKS,))],
        compiler_params=vmem(8),
        name="rim_columns",
    )(velocity)


def sums_kernel(table, v_ref, weight, vec_ref):
    span, planes, width = v_ref.shape
    rows = span // CHUNKS
    zero = jnp.zeros((planes, width), F32)

    def step(c, carry):
        a, b, s, t = carry
        for r in range(rows):
            i = c * rows + r
            v = v_ref[i]
            a = a + weight[0, pl.ds(i, 1), :] * v
            b = b + weight[1, pl.ds(i, 1), :] * v
            s = s + table[4, i] * v
            t = t + table[5, i] * v
        return (a, b, s, t)

    sums = lax.fori_loop(0, CHUNKS, step, (zero, zero, zero, zero))
    for at in range(4):
        vec_ref[at] = sums[at]
    vec_ref[4] = v_ref[0]
    vec_ref[5] = v_ref[span - 1]


def local_sums(table, velocity, weight):
    span, planes, width = velocity.shape
    return pl.pallas_call(
        sums_kernel,
        out_shape=jax.ShapeDtypeStruct((6, planes, width), F32),
        in_specs=in_smem(1) + in_vmem(2),
        out_specs=in_vmem(1)[0],
        compiler_params=vmem(8),
        cost_estimate=work(8 * velocity.size, 4 * velocity.size),
        name="local_sums",
    )(table, velocity, weight)


def slope_kernel(table, metric, v_hbm, order, out_hbm, v_ref, der, v_sem, out_sem):
    span, planes, width = v_ref.shape
    inner = span - 1
    rows = span // CHUNKS
    start_all(v_hbm, v_ref, v_sem)
    zero = jnp.zeros((planes, width), F32)
    top = jnp.where(lax.axis_index("gx") == 0, 1.0, 0.0).astype(F32)

    def forward(i, carry):
        v_low, v, slo = carry
        v_high = v_ref[i + 1]
        slo = table[0, i] * (v_high - v_low) + table[1, i] * slo
        if isinstance(i, int) and i == 0:
            slo = slo + (table[3, 0] * top) * v
        der[i] = slo
        return (v, v_high, slo)

    def down(c, carry):
        chunk_copy(v_hbm, v_ref, v_sem, c + 1).wait()
        for r in range(rows):
            carry = forward(c * rows + r, carry)
        return carry

    chunk_copy(v_hbm, v_ref, v_sem, 0).wait()
    carry = down(0, (zero, v_ref[0], zero))
    carry = lax.fori_loop(1, CHUNKS - 1, down, carry)
    for i in range(span - rows, inner):
        carry = forward(i, carry)

    def finish(i, slo, difference):
        scale = metric[i]
        return scale * slo + (scale * DIRECT) * difference

    def backward(i, slo, difference):
        slo = der[i] + table[2, i] * slo
        der[i] = finish(i, slo, difference)
        return slo

    def up(step, slo):
        c = CHUNKS - 1 - step
        for r in range(rows - 1, -1, -1):
            i = c * rows + r
            slo = backward(i, slo, v_ref[i + 1] - v_ref[i - 1])
        chunk_copy(der, out_hbm, out_sem, c).start()
        return slo

    der[inner] = finish(inner, zero, -v_ref[inner - 1])
    slo = zero
    for i in range(inner - 1, span - 1 - rows, -1):
        slo = backward(i, slo, v_ref[i + 1] - v_ref[i - 1])
    chunk_copy(der, out_hbm, out_sem, CHUNKS - 1).start()
    slo = lax.fori_loop(1, CHUNKS - 1, up, slo)
    for i in range(rows - 1, -1, -1):
        slo = backward(i, slo, v_ref[i + 1] - v_ref[i - 1] if i else v_ref[1])
    chunk_copy(der, out_hbm, out_sem, 0).start()
    for c in range(CHUNKS):
        chunk_copy(der, out_hbm, out_sem, c).wait()


def slope_solve(table, metric, velocity, order):
    return pl.pallas_call(
        slope_kernel,
        out_shape=pltpu.HBM(velocity.shape, F32),
        in_specs=in_smem(2) + in_hbm(1) + [pl.BlockSpec(memory_space=pl.ANY)],
        out_specs=in_hbm(1)[0],
        scratch_shapes=streamed(velocity.shape, 2) + [pltpu.SemaphoreType.DMA((CHUNKS,))] * 2,
        compiler_params=vmem(12),
        cost_estimate=work(12 * velocity.size, 12 * velocity.size),
        name="slope_solve",
    )(table, metric, velocity, order)


def viscous_kernel(
    v_hbm,
    line,
    before_ref,
    after_ref,
    cross_ref,
    order,
    out_hbm,
    kept,
    v_ref,
    upd,
    even,
    odd,
    v_sem,
    out_sem,
):
    span, planes, width = v_ref.shape
    inner = span - 1
    rows = span // CHUNKS
    start_all(v_hbm, v_ref, v_sem)
    lane = lane_of((planes, width))
    ahead = pltpu.roll(after_ref[...], width - 1, 1)
    even[...] = jnp.where(lax.rem(lane, 2) == 0, before_ref[...], ahead)
    odd[...] = jnp.where(lax.rem(lane, 2) == 1, before_ref[...], ahead)
    cross = jnp.broadcast_to(cross_ref[...], (planes, width))
    keep = 1.0 - 2.0 * cross
    zero = jnp.zeros((planes, width), F32)

    def forward(i, r, vis):
        v = v_ref[i]
        rim = (odd if r % 2 else even)[...]
        if r:
            rim = pltpu.roll(rim, width - r, 1)
        low = jnp.where(lane == 0, rim, pltpu.roll(v, 1, 1))
        high = jnp.where(lane == width - 1, rim, pltpu.roll(v, width - 1, 1))
        rhs = keep * v + cross * (low + high)
        vis = line[0, pl.ds(i, 1), :] * rhs + line[1, pl.ds(i, 1), :] * vis
        upd[i] = vis
        return vis

    def down(c, vis):
        chunk_copy(v_hbm, v_ref, v_sem, c).wait()
        for r in range(rows):
            vis = forward(c * rows + r, r, vis)
        even[...] = pltpu.roll(even[...], width - rows, 1)
        odd[...] = pltpu.roll(odd[...], width - rows, 1)
        return vis

    lax.fori_loop(0, CHUNKS, down, zero)

    base = (CHUNKS - KEPT) * rows

    def backward(i, vis):
        return upd[i] + line[2, pl.ds(i, 1), :] * vis

    kept[inner - base] = zero
    vis = zero
    for i in range(inner - 1, span - 1 - rows, -1):
        vis = backward(i, vis)
        kept[i - base] = vis

    def keep_chunk(step, vis):
        for r in range(rows - 1, -1, -1):
            i = (CHUNKS - 1 - step) * rows + r
            vis = backward(i, vis)
            kept[i - base] = vis
        return vis

    vis = lax.fori_loop(1, KEPT, keep_chunk, vis)
    for c in range(CHUNKS - KEPT - 1, -1, -1):
        for r in range(rows - 1, -1, -1):
            i = c * rows + r
            vis = backward(i, vis)
            upd[i] = vis
        row_copy(upd, out_hbm, out_sem, c, rows).start()
    for c in range(CHUNKS - KEPT):
        row_copy(upd, out_hbm, out_sem, c, rows).wait()


def viscous_solve(velocity, line, before, after, cross, order):
    span, planes, width = velocity.shape
    kept = KEPT * (span // CHUNKS)
    return pl.pallas_call(
        viscous_kernel,
        out_shape=(
            pltpu.HBM((span - kept, planes, width), F32),
            pltpu.VMEM((kept, planes, width), F32),
        ),
        in_specs=in_hbm(1) + in_vmem(4) + [pl.BlockSpec(memory_space=pl.ANY)],
        out_specs=tuple(in_hbm(1) + in_vmem(1)),
        scratch_shapes=streamed(velocity.shape, 2)
        + [pltpu.VMEM((planes, width), F32)] * 2
        + [pltpu.SemaphoreType.DMA((CHUNKS,))] * 2,
        compiler_params=vmem(12),
        cost_estimate=work(12 * velocity.size, 12 * velocity.size),
        name="viscous_solve",
    )(velocity, line, before, after, cross, order)


def wall_normal(value, before, after, cross):
    shape = value.shape
    lane = lane_of(shape)
    low = jnp.where(lane == 0, before, pltpu.roll(value, 1, 1))
    high = jnp.where(lane == shape[1] - 1, after, pltpu.roll(value, shape[1] - 1, 1))
    return (1.0 - 2.0 * cross) * value + cross * (low + high)


def pack_kernel(vec_ref, row_ref, before_ref, after_ref, cross_ref, out_ref, token):
    blocks = out_ref.shape[0]
    part = vec_ref.shape[1] // blocks
    cross = cross_ref[...]
    vectors = []
    for at in range(2):
        weights = row_ref[at, 0:1, :]
        before = jnp.sum(before_ref[...] * weights, axis=1, keepdims=True)
        after = jnp.sum(after_ref[...] * weights, axis=1, keepdims=True)
        vectors.append(wall_normal(vec_ref[at], before, after, cross))
    vectors += [vec_ref[at] for at in range(2, 6)]
    for at, value in enumerate(vectors):
        for m in range(blocks):
            out_ref[m, at] = value[part * m : part * (m + 1), :]
    token[...] = jnp.zeros(token.shape, F32)


def pack(vec, row, before, after, cross, blocks):
    _, planes, width = vec.shape
    part = planes // blocks
    return pl.pallas_call(
        pack_kernel,
        out_shape=(jax.ShapeDtypeStruct((blocks, 6, part, width), F32), TOKEN),
        compiler_params=vmem(8),
        name="pack_sums",
    )(vec, row, before, after, cross)


def reduced_kernel(red, weights, coef_ref, in_ref, order, out_ref, token):
    blocks, _, part, width = in_ref.shape
    slope_after, slope_before = (weights["after"], weights["before"])

    def piece(k, at):
        return in_ref[k, at]

    zero = jnp.zeros((part, width), F32)
    vis, slo = (zero, zero)
    vis_all, slo_all = ([], [])
    for k in range(blocks):
        vis_rhs = piece(k, 0)
        slo_rhs = piece(k, 2)
        if k < blocks - 1:
            vis_rhs = vis_rhs + piece(k + 1, 1)
            slo_rhs = slo_rhs + piece(k + 1, 3) + slope_after * piece(k, 5)
        else:
            slo_rhs = slo_rhs + weights["last_end"] * piece(k, 5)
        if k > 0:
            slo_rhs = slo_rhs + slope_before * piece(k - 1, 5)
        else:
            slo_rhs = slo_rhs + weights["first_end"] * piece(k, 4)
        vis = coef_ref[0, k : k + 1, :] * vis_rhs + coef_ref[1, k : k + 1, :] * vis
        slo = red[k][0] * slo_rhs + red[k][1] * slo
        vis_all.append(vis)
        slo_all.append(slo)
    vis, slo = (zero, zero)
    for k in range(blocks - 1, -1, -1):
        vis = vis_all[k] + coef_ref[2, k : k + 1, :] * vis
        slo = slo_all[k] + red[k][2] * slo
        out_ref[k, 1] = vis
        out_ref[k, 3] = slo
        if k < blocks - 1:
            out_ref[k + 1, 0] = vis
            out_ref[k + 1, 2] = slo + (BODY / ALPHA) * piece(k, 5)
        else:
            out_ref[0, 0] = zero
            out_ref[0, 2] = zero
        out_ref[k, 4] = piece(k - 1, 5) if k > 0 else zero
        out_ref[k, 5] = piece(k + 1, 4) if k < blocks - 1 else zero
    token[...] = jnp.zeros(token.shape, F32)


def reduced_solve(coef, arrived, order, red, weights):
    return pl.pallas_call(
        functools.partial(reduced_kernel, red, weights),
        out_shape=(jax.ShapeDtypeStruct(arrived.shape, F32), TOKEN),
        in_specs=in_vmem(2) + in_hbm(1),
        out_specs=tuple(in_vmem(2)),
        compiler_params=vmem(8),
        name="reduced_solve",
    )(coef, arrived, order)


def final_kernel(
    table,
    metric,
    der_in,
    upd_in,
    kept,
    edge_ref,
    spike,
    der_hbm,
    upd_hbm,
    der,
    upd,
    edges,
    der_from,
    upd_from,
    der_to,
    upd_to,
):
    span, planes, width = der.shape
    blocks = edge_ref.shape[0]
    part = planes // blocks
    rows = span // CHUNKS
    far = CHUNKS - KEPT
    for c in range(CHUNKS - 1, -1, -1):
        row_copy(der_in, der, der_from, c, rows).start()
    for c in range(far - 1, -1, -1):
        row_copy(upd_in, upd, upd_from, c, rows).start()
    for at in range(6):
        for m in range(blocks):
            edges[at, part * m : part * (m + 1), :] = edge_ref[m, at]
    vis_low, vis_high, slo_low, slo_high = (edges[at] for at in range(4))

    def viscous_rows(c, source, base):
        for r in range(rows):
            i = c * rows + r
            low = spike[0, pl.ds(i, 1), :] * vis_low
            high = spike[1, pl.ds(i, 1), :] * vis_high
            upd[i] = source[i - base] + low + high
        row_copy(upd, upd_hbm, upd_to, c, rows).start()

    def slope_rows(c):
        row_copy(der_in, der, der_from, c, rows).wait()
        for r in range(rows):
            i = c * rows + r
            scale = metric[i]
            der[i] = der[i] + (scale * table[6, i]) * slo_low + (scale * table[7, i]) * slo_high
        if isinstance(c, int) and c == 0:
            der[0] = der[0] - (metric[0] * DIRECT) * edges[4]
        if isinstance(c, int) and c == CHUNKS - 1:
            der[span - 1] = der[span - 1] + (metric[span - 1] * DIRECT) * edges[5]
        row_copy(der, der_hbm, der_to, c, rows).start()

    def near(step, carry):
        viscous_rows(CHUNKS - 1 - step, kept, far * rows)
        slope_rows(CHUNKS - 1 - step)
        return carry

    viscous_rows(CHUNKS - 1, kept, far * rows)
    slope_rows(CHUNKS - 1)
    lax.fori_loop(1, KEPT, near, 0)
    for c in range(far - 1, -1, -1):
        row_copy(upd_in, upd, upd_from, c, rows).wait()
        viscous_rows(c, upd, 0)
        slope_rows(c)
    for c in range(CHUNKS):
        row_copy(der, der_hbm, der_to, c, rows).wait()
        row_copy(upd, upd_hbm, upd_to, c, rows).wait()


def final_solve(table, metric, der, upd, kept, edge, spike):
    span, planes, width = der.shape
    result = jax.ShapeDtypeStruct(der.shape, F32)
    return pl.pallas_call(
        final_kernel,
        out_shape=(result, result),
        in_specs=in_smem(2) + in_hbm(2) + in_vmem(3),
        out_specs=tuple(in_hbm(2)),
        scratch_shapes=streamed(der.shape, 2)
        + [pltpu.VMEM((6, planes, width), F32)]
        + [pltpu.SemaphoreType.DMA((CHUNKS,))] * 4,
        compiler_params=vmem(12),
        name="final_solve",
    )(table, metric, der, upd, kept, edge, spike)


def body(velocity, metric, lower_coupling, upper_coupling, cross_diffusion):
    span, planes, width = velocity.shape
    blocks = lax.axis_size("gx")
    walls = lax.axis_size("gy")
    rows, red, weights = slope_constants(blocks, span)
    table = jnp.asarray(rows)
    cross = cross_diffusion.reshape(1, width)
    field = pltpu.with_memory_space_constraint(velocity, pltpu.HBM)
    lower = lower_coupling.reshape(blocks, span)
    upper = upper_coupling.reshape(blocks, span)
    near, first, last = rim_columns(field)
    up = [(j, j + 1) for j in range(walls - 1)]
    down = [(j + 1, j) for j in range(walls - 1)]
    before = lax.ppermute(last, "gy", up)
    after = lax.ppermute(first, "gy", down)
    line, weight, spike, row, coef = block_terms(lower, upper)
    vec = local_sums(table, near, weight)
    packed, token = pack(vec, row, before, after, cross, blocks)
    arrived = lax.all_to_all(packed, "gx", 0, 0, tiled=True)
    der = slope_solve(table, metric, field, token)
    der = pltpu.with_memory_space_constraint(der, pltpu.HBM)
    solved, token = reduced_solve(coef, arrived, der, red, weights)
    edge = lax.all_to_all(solved, "gx", 0, 0, tiled=True)
    upd, kept = viscous_solve(field, line, before, after, cross, token)
    upd = pltpu.with_memory_space_constraint(upd, pltpu.HBM)
    return final_solve(table, metric, der, upd, kept, edge, spike)


def solution(mesh):
    return jax.shard_map(
        body,
        mesh=mesh,
        in_specs=(P("gx", None, "gy"), P("gx"), P(), P(), P("gy")),
        out_specs=(P("gx", None, "gy"), P("gx", None, "gy")),
        check_vma=False,
    )
```

```python
import functools

import jax
import jax.numpy as jnp
import numpy as np
from jax import lax
from jax.experimental import pallas as pl
from jax.experimental.pallas import tpu as pltpu
from jax.sharding import PartitionSpec as P


ALPHA = 1.0 / 3.0
BODY = 25.0 / 36.0
DIRECT = 1.0 / 12.0
END = 1.0 / 36.0
LANES = 128
CHUNKS = 8
KEPT = 6
MIB = 1024 * 1024
F32 = jnp.float32
TOKEN = jax.ShapeDtypeStruct((8, LANES), F32)


@functools.lru_cache(maxsize=None)
def slope_constants(blocks, span):
    inner = span - 1
    off = -ALPHA
    fwd = np.ones(span)
    for i in range(1, inner):
        fwd[i] = 1.0 / (1.0 - off * off * fwd[i - 1])
    bwd = np.ones(span)
    for i in range(inner - 2, -1, -1):
        bwd[i] = 1.0 / (1.0 - off * off * bwd[i + 1])
    rho, mu, nu = (fwd.copy(), fwd * off, fwd * off)
    own = np.zeros(span + 2)
    acc = 1.0
    for i in range(inner - 1, -1, -1):
        own[i + 1] = off * rho[i] * acc
        acc *= mu[i]
    through = acc
    own[inner + 1] = 1.0
    first = np.zeros(span + 2)
    acc = 1.0
    for i in range(inner):
        first[i + 1] = bwd[i] * acc
        acc *= bwd[i] * off
    cross = acc
    own_v = np.zeros(span + 2)
    first_v = np.zeros(span + 2)
    for at in range(span + 2):
        low = own[at - 1] if at > 0 else 0.0
        high = own[at + 1] if at < span + 1 else 0.0
        own_v[at] = BODY * (low - high)
        low = first[at - 1] if at > 0 else 0.0
        high = first[at + 1] if at < span + 1 else 0.0
        first_v[at] = BODY * (low - high)
    sum_own = own_v[1 : span + 1].copy()
    sum_next = off * first_v[1 : span + 1]
    sum_next[0] += own_v[span + 1]
    low = off * through
    high = off * cross
    ends = off * bwd[0]
    red = []
    previous = 0.0
    for k in range(blocks):
        middle = 1.0 - off * nu[inner - 1] - (off * ends if k < blocks - 1 else 0.0)
        left = low if k > 0 else 0.0
        right = high if k < blocks - 1 else 0.0
        pivot = 1.0 / (middle - left * previous)
        red.append((pivot, pivot * left, pivot * right))
        previous = pivot * right
    lead = np.zeros(span)
    trail = np.ones(span)
    acc = 1.0
    for i in range(inner):
        acc *= bwd[i] * off
        lead[i] = acc
    acc = 1.0
    for i in range(inner - 1, -1, -1):
        acc *= nu[i]
        trail[i] = acc
    table = [rho * BODY, mu, nu, rho * END, sum_own, sum_next, lead, trail]
    rows = np.stack(table).astype(np.float32)
    weights = {
        "before": float(own_v[0]),
        "after": float(off * first_v[0]),
        "first_end": float(own[1] * END),
        "last_end": float(-own[inner + 1] * END),
    }
    return rows, red, weights


def lane_of(shape):
    return lax.broadcasted_iota(jnp.int32, shape, len(shape) - 1)


def vmem(mib):
    return pltpu.CompilerParams(vmem_limit_bytes=mib * MIB)


def work(ops, reads):
    return pl.CostEstimate(flops=ops, bytes_accessed=reads, transcendentals=0)


def in_vmem(count):
    return [pl.BlockSpec(memory_space=pltpu.VMEM)] * count


def in_hbm(count):
    return [pl.BlockSpec(memory_space=pltpu.HBM)] * count


def in_smem(count):
    return [pl.BlockSpec(memory_space=pltpu.SMEM)] * count


def viscous_terms(
    blocks,
    low_ref,
    up_ref,
    line_ref,
    weight_ref,
    spike_ref,
    row_ref,
    red_ref,
    kap,
    dnow,
    dpre,
    enow,
    enxt,
    factor,
    chain,
    turn,
):
    span = line_ref.shape[1]
    inner = span - 1
    index = lax.axis_index("gx")
    filler = jnp.ones((LANES - blocks, span), F32)
    lower = jnp.transpose(jnp.concatenate([low_ref[...], filler], 0))
    upper = jnp.transpose(jnp.concatenate([up_ref[...], filler], 0))
    row = lax.broadcasted_iota(jnp.int32, (span, LANES), 0)
    lane = lane_of((span, LANES))
    scale = 1.0 / (1.0 + lower + upper)
    alpha = jnp.where((row == 0) & (lane == 0), 0.0, lower * scale)
    gamma = jnp.where((row == inner) & (lane == blocks - 1), 0.0, upper * scale)
    kap[...] = alpha * pltpu.roll(gamma, 1, 0)
    one = jnp.ones((1, LANES), F32)
    dnow[0:1, :] = one
    dpre[0:1, :] = one
    enow[inner - 1 : inner, :] = one
    enxt[inner - 1 : inner, :] = one
    for ref in (dnow, dpre, enow, enxt):
        ref[inner:span, :] = one
    d1, d2, e1, e2 = (one, one, one, one)
    for i in range(1, inner):
        d0 = d1 - kap[i : i + 1, :] * d2
        dpre[i : i + 1, :] = d1
        dnow[i : i + 1, :] = d0
        d2, d1 = (d1, d0)
        j = inner - 1 - i
        e0 = e1 - kap[j + 1 : j + 2, :] * e2
        enxt[j : j + 1, :] = e1
        enow[j : j + 1, :] = e0
        e2, e1 = (e1, e0)
    fwd = dpre[...] / dnow[...]
    bwd = enxt[...] / enow[...]
    rho, mu, nu = (fwd * scale, fwd * alpha, fwd * gamma)
    factor[0] = mu
    factor[1] = bwd * gamma
    factor[2] = bwd * alpha
    factor[3] = nu
    h_acc, g_acc, l_acc, t_acc = (one, one, one, one)
    for i in range(inner):
        j = inner - 1 - i
        chain[0, j : j + 1, :] = h_acc
        chain[1, i : i + 1, :] = g_acc
        h_acc = h_acc * factor[0, j : j + 1, :]
        g_acc = g_acc * factor[1, i : i + 1, :]
        l_acc = l_acc * factor[2, i : i + 1, :]
        t_acc = t_acc * factor[3, j : j + 1, :]
        chain[2, i : i + 1, :] = l_acc
        chain[3, j : j + 1, :] = t_acc
    zero = jnp.zeros((1, LANES), F32)
    chain[0, inner:span, :] = one
    chain[1, inner:span, :] = zero
    chain[2, inner:span, :] = zero
    chain[3, inner:span, :] = one
    alpha_end = alpha[inner:span, :]
    gamma_end = gamma[inner:span, :]
    own = jnp.where(row == inner, 1.0, alpha_end * chain[0]) * rho
    first = bwd * scale * chain[1] * pltpu.roll(gamma_end, 1, 1)
    inflow = bwd[0:1, :] * alpha[0:1, :]
    middle = (
        1.0
        - alpha_end * nu[inner - 1 : inner, :]
        - gamma_end * pltpu.roll(inflow, LANES - 1, 1)
    )
    scale_red = 1.0 / middle
    left = alpha_end * h_acc * scale_red
    right = gamma_end * pltpu.roll(t_acc, LANES - 1, 1) * scale_red
    product = left * pltpu.roll(right, 1, 1)
    for at, value in enumerate((scale_red, left, right, product)):
        turn[at] = jnp.transpose(jnp.broadcast_to(value, (LANES, LANES)))
    d1, d2 = (one, one)
    for k in range(blocks):
        if k == 0:
            ratio = one
        else:
            d0 = d1 - turn[3, k : k + 1, :] * d2
            ratio = d1 / d0
            d2, d1 = (d1, d0)
        for at in range(3):
            red_ref[at, k : k + 1, :] = turn[at, k : k + 1, :] * ratio

    def mine(value):
        column = jnp.sum(jnp.where(lane == index, value, 0.0), axis=1, keepdims=True)
        return jnp.broadcast_to(column, (span, LANES))

    for at, value in enumerate((rho, mu, nu)):
        turn[at] = jnp.transpose(value)
        line_ref[at : at + 1, :] = turn[at, pl.ds(index, 1), :]
    for at in range(2):
        turn[at] = jnp.transpose(chain[2 + at])
        spike_ref[at : at + 1, :] = turn[at, pl.ds(index, 1), :]
    for at, value in enumerate((own, first)):
        here = mine(value)
        weight_ref[at] = here
        row_ref[at] = jnp.transpose(here)[0:8, :]


def chunk_copy(source, target, sem, c):
    rows = source.shape[0] // CHUNKS
    where = pl.ds(c * rows, rows)
    return pltpu.make_async_copy(source.at[where], target.at[where], sem.at[c])


def row_copy(source, target, sem, c, rows):
    where = pl.ds(c * rows, rows)
    return pltpu.make_async_copy(source.at[where], target.at[where], sem.at[c])


def start_all(source, target, sem):
    for c in range(CHUNKS):
        chunk_copy(source, target, sem, c).start()


def streamed(shape, count):
    return [pltpu.VMEM(shape, F32)] * count


def block_terms(lower, upper):
    blocks, span = lower.shape
    square = pltpu.VMEM((span, LANES), F32)
    four = pltpu.VMEM((4, span, LANES), F32)
    return pl.pallas_call(
        functools.partial(viscous_terms, blocks),
        out_shape=(
            jax.ShapeDtypeStruct((3, span), F32),
            jax.ShapeDtypeStruct((2, span, LANES), F32),
            jax.ShapeDtypeStruct((2, span), F32),
            jax.ShapeDtypeStruct((2, 8, span), F32),
            jax.ShapeDtypeStruct((3, blocks, LANES), F32),
        ),
        in_specs=in_vmem(2),
        out_specs=tuple(in_vmem(5)),
        scratch_shapes=[square] * 5
        + [four, four, pltpu.VMEM((4, LANES, LANES), F32)],
        compiler_params=vmem(8),
        cost_estimate=work(4 * MIB, MIB),
        name="block_terms",
    )(lower, upper)


def rim_kernel(v_hbm, v_ref, first_ref, last_ref, v_sem):
    span, planes, width = v_ref.shape
    rows = span // CHUNKS
    start_all(v_hbm, v_ref, v_sem)
    lane = lane_of((planes, width))
    zero = jnp.zeros((planes, width), F32)

    def step(c, carry):
        first, last = carry
        chunk_copy(v_hbm, v_ref, v_sem, c).wait()
        for r in range(rows):
            i = c * rows + r
            turned = pltpu.roll(v_ref[i], i, 1)
            first = jnp.where(lane == i, turned, first)
            last = jnp.where(lane == lax.rem(i + width - 1, width), turned, last)
        return (first, last)

    first, last = lax.fori_loop(0, CHUNKS, step, (zero, zero))
    first_ref[...] = first
    last_ref[...] = pltpu.roll(last, 1, 1)


def rim_columns(velocity):
    span, planes, width = velocity.shape
    column = jax.ShapeDtypeStruct((planes, width), F32)
    return pl.pallas_call(
        rim_kernel,
        out_shape=(pltpu.VMEM(velocity.shape, F32), column, column),
        in_specs=in_hbm(1),
        out_specs=tuple(in_vmem(3)),
        scratch_shapes=[pltpu.SemaphoreType.DMA((CHUNKS,))],
        compiler_params=vmem(8),
        name="rim_columns",
    )(velocity)


def sums_kernel(table, v_ref, weight, vec_ref):
    span, planes, width = v_ref.shape
    rows = span // CHUNKS
    zero = jnp.zeros((planes, width), F32)

    def step(c, carry):
        a, b, s, t = carry
        for r in range(rows):
            i = c * rows + r
            v = v_ref[i]
            a = a + weight[0, pl.ds(i, 1), :] * v
            b = b + weight[1, pl.ds(i, 1), :] * v
            s = s + table[4, i] * v
            t = t + table[5, i] * v
        return (a, b, s, t)

    sums = lax.fori_loop(0, CHUNKS, step, (zero, zero, zero, zero))
    for at in range(4):
        vec_ref[at] = sums[at]
    vec_ref[4] = v_ref[0]
    vec_ref[5] = v_ref[span - 1]


def local_sums(table, velocity, weight):
    span, planes, width = velocity.shape
    return pl.pallas_call(
        sums_kernel,
        out_shape=jax.ShapeDtypeStruct((6, planes, width), F32),
        in_specs=in_smem(1) + in_vmem(2),
        out_specs=in_vmem(1)[0],
        compiler_params=vmem(8),
        cost_estimate=work(8 * velocity.size, 4 * velocity.size),
        name="local_sums",
    )(table, velocity, weight)


def slope_kernel(table, metric, v_hbm, order, out_hbm, v_ref, der, v_sem, out_sem):
    span, planes, width = v_ref.shape
    inner = span - 1
    rows = span // CHUNKS
    start_all(v_hbm, v_ref, v_sem)
    zero = jnp.zeros((planes, width), F32)
    top = jnp.where(lax.axis_index("gx") == 0, 1.0, 0.0).astype(F32)

    def forward(i, carry):
        v_low, v, slo = carry
        v_high = v_ref[i + 1]
        slo = table[0, i] * (v_high - v_low) + table[1, i] * slo
        if isinstance(i, int) and i == 0:
            slo = slo + (table[3, 0] * top) * v
        der[i] = slo
        return (v, v_high, slo)

    def down(c, carry):
        chunk_copy(v_hbm, v_ref, v_sem, c + 1).wait()
        for r in range(rows):
            carry = forward(c * rows + r, carry)
        return carry

    chunk_copy(v_hbm, v_ref, v_sem, 0).wait()
    carry = down(0, (zero, v_ref[0], zero))
    carry = lax.fori_loop(1, CHUNKS - 1, down, carry)
    for i in range(span - rows, inner):
        carry = forward(i, carry)

    def finish(i, slo, difference):
        scale = metric[i]
        return scale * slo + (scale * DIRECT) * difference

    def backward(i, slo, difference):
        slo = der[i] + table[2, i] * slo
        der[i] = finish(i, slo, difference)
        return slo

    def up(step, slo):
        c = CHUNKS - 1 - step
        for r in range(rows - 1, -1, -1):
            i = c * rows + r
            slo = backward(i, slo, v_ref[i + 1] - v_ref[i - 1])
        chunk_copy(der, out_hbm, out_sem, c).start()
        return slo

    der[inner] = finish(inner, zero, -v_ref[inner - 1])
    slo = zero
    for i in range(inner - 1, span - 1 - rows, -1):
        slo = backward(i, slo, v_ref[i + 1] - v_ref[i - 1])
    chunk_copy(der, out_hbm, out_sem, CHUNKS - 1).start()
    slo = lax.fori_loop(1, CHUNKS - 1, up, slo)
    for i in range(rows - 1, -1, -1):
        slo = backward(i, slo, v_ref[i + 1] - v_ref[i - 1] if i else v_ref[1])
    chunk_copy(der, out_hbm, out_sem, 0).start()
    for c in range(CHUNKS):
        chunk_copy(der, out_hbm, out_sem, c).wait()


def slope_solve(table, metric, velocity, order):
    return pl.pallas_call(
        slope_kernel,
        out_shape=pltpu.HBM(velocity.shape, F32),
        in_specs=in_smem(2) + in_hbm(1) + [pl.BlockSpec(memory_space=pl.ANY)],
        out_specs=in_hbm(1)[0],
        scratch_shapes=streamed(velocity.shape, 2) + [pltpu.SemaphoreType.DMA((CHUNKS,))] * 2,
        compiler_params=vmem(12),
        cost_estimate=work(12 * velocity.size, 12 * velocity.size),
        name="slope_solve",
    )(table, metric, velocity, order)


def viscous_kernel(
    v_hbm,
    line,
    before_ref,
    after_ref,
    cross_ref,
    order,
    out_hbm,
    kept,
    v_ref,
    upd,
    even,
    odd,
    v_sem,
    out_sem,
):
    span, planes, width = v_ref.shape
    inner = span - 1
    rows = span // CHUNKS
    start_all(v_hbm, v_ref, v_sem)
    lane = lane_of((planes, width))
    ahead = pltpu.roll(after_ref[...], width - 1, 1)
    even[...] = jnp.where(lax.rem(lane, 2) == 0, before_ref[...], ahead)
    odd[...] = jnp.where(lax.rem(lane, 2) == 1, before_ref[...], ahead)
    cross = jnp.broadcast_to(cross_ref[...], (planes, width))
    keep = 1.0 - 2.0 * cross
    zero = jnp.zeros((planes, width), F32)

    def forward(i, r, vis):
        v = v_ref[i]
        rim = (odd if r % 2 else even)[...]
        if r:
            rim = pltpu.roll(rim, width - r, 1)
        low = jnp.where(lane == 0, rim, pltpu.roll(v, 1, 1))
        high = jnp.where(lane == width - 1, rim, pltpu.roll(v, width - 1, 1))
        rhs = keep * v + cross * (low + high)
        vis = line[0, i] * rhs + line[1, i] * vis
        upd[i] = vis
        return vis

    def down(c, vis):
        chunk_copy(v_hbm, v_ref, v_sem, c).wait()
        for r in range(rows):
            vis = forward(c * rows + r, r, vis)
        even[...] = pltpu.roll(even[...], width - rows, 1)
        odd[...] = pltpu.roll(odd[...], width - rows, 1)
        return vis

    lax.fori_loop(0, CHUNKS, down, zero)

    base = (CHUNKS - KEPT) * rows

    def backward(i, vis):
        return upd[i] + line[2, i] * vis

    kept[inner - base] = zero
    vis = zero
    for i in range(inner - 1, span - 1 - rows, -1):
        vis = backward(i, vis)
        kept[i - base] = vis

    def keep_chunk(step, vis):
        for r in range(rows - 1, -1, -1):
            i = (CHUNKS - 1 - step) * rows + r
            vis = backward(i, vis)
            kept[i - base] = vis
        return vis

    vis = lax.fori_loop(1, KEPT, keep_chunk, vis)
    for c in range(CHUNKS - KEPT - 1, -1, -1):
        for r in range(rows - 1, -1, -1):
            i = c * rows + r
            vis = backward(i, vis)
            upd[i] = vis
        row_copy(upd, out_hbm, out_sem, c, rows).start()
    for c in range(CHUNKS - KEPT):
        row_copy(upd, out_hbm, out_sem, c, rows).wait()


def viscous_solve(velocity, line, before, after, cross, order):
    span, planes, width = velocity.shape
    kept = KEPT * (span // CHUNKS)
    return pl.pallas_call(
        viscous_kernel,
        out_shape=(
            pltpu.HBM((span - kept, planes, width), F32),
            pltpu.VMEM((kept, planes, width), F32),
        ),
        in_specs=in_hbm(1) + in_smem(1) + in_vmem(3) + [pl.BlockSpec(memory_space=pl.ANY)],
        out_specs=tuple(in_hbm(1) + in_vmem(1)),
        scratch_shapes=streamed(velocity.shape, 2)
        + [pltpu.VMEM((planes, width), F32)] * 2
        + [pltpu.SemaphoreType.DMA((CHUNKS,))] * 2,
        compiler_params=vmem(12),
        cost_estimate=work(12 * velocity.size, 12 * velocity.size),
        name="viscous_solve",
    )(velocity, line, before, after, cross, order)


def wall_normal(value, before, after, cross):
    shape = value.shape
    lane = lane_of(shape)
    low = jnp.where(lane == 0, before, pltpu.roll(value, 1, 1))
    high = jnp.where(lane == shape[1] - 1, after, pltpu.roll(value, shape[1] - 1, 1))
    return (1.0 - 2.0 * cross) * value + cross * (low + high)


def pack_kernel(vec_ref, row_ref, before_ref, after_ref, cross_ref, out_ref, token):
    blocks = out_ref.shape[0]
    part = vec_ref.shape[1] // blocks
    cross = cross_ref[...]
    vectors = []
    for at in range(2):
        weights = row_ref[at, 0:1, :]
        before = jnp.sum(before_ref[...] * weights, axis=1, keepdims=True)
        after = jnp.sum(after_ref[...] * weights, axis=1, keepdims=True)
        vectors.append(wall_normal(vec_ref[at], before, after, cross))
    vectors += [vec_ref[at] for at in range(2, 6)]
    for at, value in enumerate(vectors):
        for m in range(blocks):
            out_ref[m, at] = value[part * m : part * (m + 1), :]
    token[...] = jnp.zeros(token.shape, F32)


def pack(vec, row, before, after, cross, blocks):
    _, planes, width = vec.shape
    part = planes // blocks
    return pl.pallas_call(
        pack_kernel,
        out_shape=(jax.ShapeDtypeStruct((blocks, 6, part, width), F32), TOKEN),
        compiler_params=vmem(8),
        name="pack_sums",
    )(vec, row, before, after, cross)


def reduced_kernel(red, weights, coef_ref, in_ref, order, out_ref, token):
    blocks, _, part, width = in_ref.shape
    slope_after, slope_before = (weights["after"], weights["before"])

    def piece(k, at):
        return in_ref[k, at]

    zero = jnp.zeros((part, width), F32)
    vis, slo = (zero, zero)
    vis_all, slo_all = ([], [])
    for k in range(blocks):
        vis_rhs = piece(k, 0)
        slo_rhs = piece(k, 2)
        if k < blocks - 1:
            vis_rhs = vis_rhs + piece(k + 1, 1)
            slo_rhs = slo_rhs + piece(k + 1, 3) + slope_after * piece(k, 5)
        else:
            slo_rhs = slo_rhs + weights["last_end"] * piece(k, 5)
        if k > 0:
            slo_rhs = slo_rhs + slope_before * piece(k - 1, 5)
        else:
            slo_rhs = slo_rhs + weights["first_end"] * piece(k, 4)
        vis = coef_ref[0, k : k + 1, :] * vis_rhs + coef_ref[1, k : k + 1, :] * vis
        slo = red[k][0] * slo_rhs + red[k][1] * slo
        vis_all.append(vis)
        slo_all.append(slo)
    vis, slo = (zero, zero)
    for k in range(blocks - 1, -1, -1):
        vis = vis_all[k] + coef_ref[2, k : k + 1, :] * vis
        slo = slo_all[k] + red[k][2] * slo
        out_ref[k, 1] = vis
        out_ref[k, 3] = slo
        if k < blocks - 1:
            out_ref[k + 1, 0] = vis
            out_ref[k + 1, 2] = slo + (BODY / ALPHA) * piece(k, 5)
        else:
            out_ref[0, 0] = zero
            out_ref[0, 2] = zero
        out_ref[k, 4] = piece(k - 1, 5) if k > 0 else zero
        out_ref[k, 5] = piece(k + 1, 4) if k < blocks - 1 else zero
    token[...] = jnp.zeros(token.shape, F32)


def reduced_solve(coef, arrived, order, red, weights):
    return pl.pallas_call(
        functools.partial(reduced_kernel, red, weights),
        out_shape=(jax.ShapeDtypeStruct(arrived.shape, F32), TOKEN),
        in_specs=in_vmem(2) + in_hbm(1),
        out_specs=tuple(in_vmem(2)),
        compiler_params=vmem(8),
        name="reduced_solve",
    )(coef, arrived, order)


def final_kernel(
    table,
    metric,
    der_in,
    upd_in,
    kept,
    edge_ref,
    spike,
    der_hbm,
    upd_hbm,
    der,
    upd,
    edges,
    der_from,
    upd_from,
    der_to,
    upd_to,
):
    span, planes, width = der.shape
    blocks = edge_ref.shape[0]
    part = planes // blocks
    rows = span // CHUNKS
    far = CHUNKS - KEPT
    for c in range(CHUNKS - 1, -1, -1):
        row_copy(der_in, der, der_from, c, rows).start()
    for c in range(far - 1, -1, -1):
        row_copy(upd_in, upd, upd_from, c, rows).start()
    for at in range(6):
        for m in range(blocks):
            edges[at, part * m : part * (m + 1), :] = edge_ref[m, at]
    vis_low, vis_high, slo_low, slo_high = (edges[at] for at in range(4))

    def viscous_rows(c, source, base):
        for r in range(rows):
            i = c * rows + r
            low = spike[0, i] * vis_low
            high = spike[1, i] * vis_high
            upd[i] = source[i - base] + low + high
        row_copy(upd, upd_hbm, upd_to, c, rows).start()

    def slope_rows(c):
        row_copy(der_in, der, der_from, c, rows).wait()
        for r in range(rows):
            i = c * rows + r
            scale = metric[i]
            der[i] = der[i] + (scale * table[6, i]) * slo_low + (scale * table[7, i]) * slo_high
        if isinstance(c, int) and c == 0:
            der[0] = der[0] - (metric[0] * DIRECT) * edges[4]
        if isinstance(c, int) and c == CHUNKS - 1:
            der[span - 1] = der[span - 1] + (metric[span - 1] * DIRECT) * edges[5]
        row_copy(der, der_hbm, der_to, c, rows).start()

    def near(step, carry):
        viscous_rows(CHUNKS - 1 - step, kept, far * rows)
        slope_rows(CHUNKS - 1 - step)
        return carry

    viscous_rows(CHUNKS - 1, kept, far * rows)
    slope_rows(CHUNKS - 1)
    lax.fori_loop(1, KEPT, near, 0)
    for c in range(far - 1, -1, -1):
        row_copy(upd_in, upd, upd_from, c, rows).wait()
        viscous_rows(c, upd, 0)
        slope_rows(c)
    for c in range(CHUNKS):
        row_copy(der, der_hbm, der_to, c, rows).wait()
        row_copy(upd, upd_hbm, upd_to, c, rows).wait()


def final_solve(table, metric, der, upd, kept, edge, spike):
    span, planes, width = der.shape
    result = jax.ShapeDtypeStruct(der.shape, F32)
    return pl.pallas_call(
        final_kernel,
        out_shape=(result, result),
        in_specs=in_smem(2) + in_hbm(2) + in_vmem(2) + in_smem(1),
        out_specs=tuple(in_hbm(2)),
        scratch_shapes=streamed(der.shape, 2)
        + [pltpu.VMEM((6, planes, width), F32)]
        + [pltpu.SemaphoreType.DMA((CHUNKS,))] * 4,
        compiler_params=vmem(12),
        name="final_solve",
    )(table, metric, der, upd, kept, edge, spike)


def body(velocity, metric, lower_coupling, upper_coupling, cross_diffusion):
    span, planes, width = velocity.shape
    blocks = lax.axis_size("gx")
    walls = lax.axis_size("gy")
    rows, red, weights = slope_constants(blocks, span)
    table = jnp.asarray(rows)
    cross = cross_diffusion.reshape(1, width)
    field = pltpu.with_memory_space_constraint(velocity, pltpu.HBM)
    lower = lower_coupling.reshape(blocks, span)
    upper = upper_coupling.reshape(blocks, span)
    near, first, last = rim_columns(field)
    up = [(j, j + 1) for j in range(walls - 1)]
    down = [(j + 1, j) for j in range(walls - 1)]
    before = lax.ppermute(last, "gy", up)
    after = lax.ppermute(first, "gy", down)
    line, weight, spike, row, coef = block_terms(lower, upper)
    vec = local_sums(table, near, weight)
    packed, token = pack(vec, row, before, after, cross, blocks)
    arrived = lax.all_to_all(packed, "gx", 0, 0, tiled=True)
    der = slope_solve(table, metric, field, token)
    der = pltpu.with_memory_space_constraint(der, pltpu.HBM)
    solved, token = reduced_solve(coef, arrived, der, red, weights)
    edge = lax.all_to_all(solved, "gx", 0, 0, tiled=True)
    upd, kept = viscous_solve(field, line, before, after, cross, token)
    upd = pltpu.with_memory_space_constraint(upd, pltpu.HBM)
    return final_solve(table, metric, der, upd, kept, edge, spike)


def solution(mesh):
    return jax.shard_map(
        body,
        mesh=mesh,
        in_specs=(P("gx", None, "gy"), P("gx"), P(), P(), P("gy")),
        out_specs=(P("gx", None, "gy"), P("gx", None, "gy")),
        check_vma=False,
    )
```

```python
import functools

import jax
import jax.numpy as jnp
import numpy as np
from jax import lax
from jax.experimental import pallas as pl
from jax.experimental.pallas import tpu as pltpu
from jax.sharding import PartitionSpec as P


ALPHA = 1.0 / 3.0
BODY = 25.0 / 36.0
DIRECT = 1.0 / 12.0
END = 1.0 / 36.0
LANES = 128
CHUNKS = 8
KEPT = 6
MIB = 1024 * 1024
F32 = jnp.float32
TOKEN = jax.ShapeDtypeStruct((8, LANES), F32)


@functools.lru_cache(maxsize=None)
def slope_constants(blocks, span):
    inner = span - 1
    off = -ALPHA
    fwd = np.ones(span)
    for i in range(1, inner):
        fwd[i] = 1.0 / (1.0 - off * off * fwd[i - 1])
    bwd = np.ones(span)
    for i in range(inner - 2, -1, -1):
        bwd[i] = 1.0 / (1.0 - off * off * bwd[i + 1])
    rho, mu, nu = (fwd.copy(), fwd * off, fwd * off)
    own = np.zeros(span + 2)
    acc = 1.0
    for i in range(inner - 1, -1, -1):
        own[i + 1] = off * rho[i] * acc
        acc *= mu[i]
    through = acc
    own[inner + 1] = 1.0
    first = np.zeros(span + 2)
    acc = 1.0
    for i in range(inner):
        first[i + 1] = bwd[i] * acc
        acc *= bwd[i] * off
    cross = acc
    own_v = np.zeros(span + 2)
    first_v = np.zeros(span + 2)
    for at in range(span + 2):
        low = own[at - 1] if at > 0 else 0.0
        high = own[at + 1] if at < span + 1 else 0.0
        own_v[at] = BODY * (low - high)
        low = first[at - 1] if at > 0 else 0.0
        high = first[at + 1] if at < span + 1 else 0.0
        first_v[at] = BODY * (low - high)
    sum_own = own_v[1 : span + 1].copy()
    sum_next = off * first_v[1 : span + 1]
    sum_next[0] += own_v[span + 1]
    low = off * through
    high = off * cross
    ends = off * bwd[0]
    red = []
    previous = 0.0
    for k in range(blocks):
        middle = 1.0 - off * nu[inner - 1] - (off * ends if k < blocks - 1 else 0.0)
        left = low if k > 0 else 0.0
        right = high if k < blocks - 1 else 0.0
        pivot = 1.0 / (middle - left * previous)
        red.append((pivot, pivot * left, pivot * right))
        previous = pivot * right
    lead = np.zeros(span)
    trail = np.ones(span)
    acc = 1.0
    for i in range(inner):
        acc *= bwd[i] * off
        lead[i] = acc
    acc = 1.0
    for i in range(inner - 1, -1, -1):
        acc *= nu[i]
        trail[i] = acc
    table = [rho * BODY, mu, nu, rho * END, sum_own, sum_next, lead, trail]
    rows = np.stack(table).astype(np.float32)
    weights = {
        "before": float(own_v[0]),
        "after": float(off * first_v[0]),
        "first_end": float(own[1] * END),
        "last_end": float(-own[inner + 1] * END),
    }
    return rows, red, weights


def lane_of(shape):
    return lax.broadcasted_iota(jnp.int32, shape, len(shape) - 1)


def vmem(mib):
    return pltpu.CompilerParams(vmem_limit_bytes=mib * MIB)


def work(ops, reads):
    return pl.CostEstimate(flops=ops, bytes_accessed=reads, transcendentals=0)


def in_vmem(count):
    return [pl.BlockSpec(memory_space=pltpu.VMEM)] * count


def in_hbm(count):
    return [pl.BlockSpec(memory_space=pltpu.HBM)] * count


def in_smem(count):
    return [pl.BlockSpec(memory_space=pltpu.SMEM)] * count


def viscous_terms(
    blocks,
    low_ref,
    up_ref,
    line_ref,
    weight_ref,
    spike_ref,
    row_ref,
    red_ref,
    kap,
    dnow,
    dpre,
    enow,
    enxt,
    factor,
    chain,
    turn,
):
    span = line_ref.shape[1]
    inner = span - 1
    index = lax.axis_index("gx")
    filler = jnp.ones((LANES - blocks, span), F32)
    lower = jnp.transpose(jnp.concatenate([low_ref[...], filler], 0))
    upper = jnp.transpose(jnp.concatenate([up_ref[...], filler], 0))
    row = lax.broadcasted_iota(jnp.int32, (span, LANES), 0)
    lane = lane_of((span, LANES))
    scale = 1.0 / (1.0 + lower + upper)
    alpha = jnp.where((row == 0) & (lane == 0), 0.0, lower * scale)
    gamma = jnp.where((row == inner) & (lane == blocks - 1), 0.0, upper * scale)
    kap[...] = alpha * pltpu.roll(gamma, 1, 0)
    one = jnp.ones((1, LANES), F32)
    dnow[0:1, :] = one
    dpre[0:1, :] = one
    enow[inner - 1 : inner, :] = one
    enxt[inner - 1 : inner, :] = one
    for ref in (dnow, dpre, enow, enxt):
        ref[inner:span, :] = one
    d1, d2, e1, e2 = (one, one, one, one)
    for i in range(1, inner):
        d0 = d1 - kap[i : i + 1, :] * d2
        dpre[i : i + 1, :] = d1
        dnow[i : i + 1, :] = d0
        d2, d1 = (d1, d0)
        j = inner - 1 - i
        e0 = e1 - kap[j + 1 : j + 2, :] * e2
        enxt[j : j + 1, :] = e1
        enow[j : j + 1, :] = e0
        e2, e1 = (e1, e0)
    fwd = dpre[...] / dnow[...]
    bwd = enxt[...] / enow[...]
    rho, mu, nu = (fwd * scale, fwd * alpha, fwd * gamma)
    factor[0] = mu
    factor[1] = bwd * gamma
    factor[2] = bwd * alpha
    factor[3] = nu
    h_acc, g_acc, l_acc, t_acc = (one, one, one, one)
    for i in range(inner):
        j = inner - 1 - i
        chain[0, j : j + 1, :] = h_acc
        chain[1, i : i + 1, :] = g_acc
        h_acc = h_acc * factor[0, j : j + 1, :]
        g_acc = g_acc * factor[1, i : i + 1, :]
        l_acc = l_acc * factor[2, i : i + 1, :]
        t_acc = t_acc * factor[3, j : j + 1, :]
        chain[2, i : i + 1, :] = l_acc
        chain[3, j : j + 1, :] = t_acc
    zero = jnp.zeros((1, LANES), F32)
    chain[0, inner:span, :] = one
    chain[1, inner:span, :] = zero
    chain[2, inner:span, :] = zero
    chain[3, inner:span, :] = one
    alpha_end = alpha[inner:span, :]
    gamma_end = gamma[inner:span, :]
    own = jnp.where(row == inner, 1.0, alpha_end * chain[0]) * rho
    first = bwd * scale * chain[1] * pltpu.roll(gamma_end, 1, 1)
    inflow = bwd[0:1, :] * alpha[0:1, :]
    middle = (
        1.0
        - alpha_end * nu[inner - 1 : inner, :]
        - gamma_end * pltpu.roll(inflow, LANES - 1, 1)
    )
    scale_red = 1.0 / middle
    left = alpha_end * h_acc * scale_red
    right = gamma_end * pltpu.roll(t_acc, LANES - 1, 1) * scale_red
    product = left * pltpu.roll(right, 1, 1)
    for at, value in enumerate((scale_red, left, right, product)):
        turn[at] = jnp.transpose(jnp.broadcast_to(value, (LANES, LANES)))
    d1, d2 = (one, one)
    for k in range(blocks):
        if k == 0:
            ratio = one
        else:
            d0 = d1 - turn[3, k : k + 1, :] * d2
            ratio = d1 / d0
            d2, d1 = (d1, d0)
        for at in range(3):
            red_ref[at, k : k + 1, :] = turn[at, k : k + 1, :] * ratio

    def mine(value):
        column = jnp.sum(jnp.where(lane == index, value, 0.0), axis=1, keepdims=True)
        return jnp.broadcast_to(column, (span, LANES))

    for at, value in enumerate((rho, mu, nu)):
        turn[at] = jnp.transpose(value)
        line_ref[at : at + 1, :] = turn[at, pl.ds(index, 1), :]
    for at in range(2):
        turn[at] = jnp.transpose(chain[2 + at])
        spike_ref[at : at + 1, :] = turn[at, pl.ds(index, 1), :]
    for at, value in enumerate((own, first)):
        here = mine(value)
        weight_ref[at] = here
        row_ref[at] = jnp.transpose(here)[0:8, :]


def chunk_copy(source, target, sem, c):
    rows = source.shape[0] // CHUNKS
    where = pl.ds(c * rows, rows)
    return pltpu.make_async_copy(source.at[where], target.at[where], sem.at[c])


def row_copy(source, target, sem, c, rows):
    where = pl.ds(c * rows, rows)
    return pltpu.make_async_copy(source.at[where], target.at[where], sem.at[c])


def start_all(source, target, sem):
    for c in range(CHUNKS):
        chunk_copy(source, target, sem, c).start()


def streamed(shape, count):
    return [pltpu.VMEM(shape, F32)] * count


def block_terms(lower, upper):
    blocks, span = lower.shape
    square = pltpu.VMEM((span, LANES), F32)
    four = pltpu.VMEM((4, span, LANES), F32)
    return pl.pallas_call(
        functools.partial(viscous_terms, blocks),
        out_shape=(
            jax.ShapeDtypeStruct((3, span), F32),
            jax.ShapeDtypeStruct((2, span, LANES), F32),
            jax.ShapeDtypeStruct((2, span), F32),
            jax.ShapeDtypeStruct((2, 8, span), F32),
            jax.ShapeDtypeStruct((3, blocks, LANES), F32),
        ),
        in_specs=in_vmem(2),
        out_specs=tuple(in_vmem(5)),
        scratch_shapes=[square] * 5
        + [four, four, pltpu.VMEM((4, LANES, LANES), F32)],
        compiler_params=vmem(8),
        cost_estimate=work(4 * MIB, MIB),
        name="block_terms",
    )(lower, upper)


def rim_kernel(v_hbm, v_ref, first_ref, last_ref, v_sem):
    span, planes, width = v_ref.shape
    rows = span // CHUNKS
    start_all(v_hbm, v_ref, v_sem)
    lane = lane_of((planes, width))
    zero = jnp.zeros((planes, width), F32)

    def step(c, carry):
        first, last = carry
        chunk_copy(v_hbm, v_ref, v_sem, c).wait()
        for r in range(rows):
            i = c * rows + r
            turned = pltpu.roll(v_ref[i], i, 1)
            first = jnp.where(lane == i, turned, first)
            last = jnp.where(lane == lax.rem(i + width - 1, width), turned, last)
        return (first, last)

    first, last = lax.fori_loop(0, CHUNKS, step, (zero, zero))
    first_ref[...] = first
    last_ref[...] = pltpu.roll(last, 1, 1)


def rim_columns(velocity):
    span, planes, width = velocity.shape
    column = jax.ShapeDtypeStruct((planes, width), F32)
    return pl.pallas_call(
        rim_kernel,
        out_shape=(pltpu.VMEM(velocity.shape, F32), column, column),
        in_specs=in_hbm(1),
        out_specs=tuple(in_vmem(3)),
        scratch_shapes=[pltpu.SemaphoreType.DMA((CHUNKS,))],
        compiler_params=vmem(8),
        name="rim_columns",
    )(velocity)


def sums_kernel(table, v_ref, weight, vec_ref):
    span, planes, width = v_ref.shape
    rows = span // CHUNKS
    zero = jnp.zeros((planes, width), F32)

    def step(c, carry):
        a, b, s, t = carry
        for r in range(rows):
            i = c * rows + r
            v = v_ref[i]
            a = a + weight[0, pl.ds(i, 1), :] * v
            b = b + weight[1, pl.ds(i, 1), :] * v
            s = s + table[4, i] * v
            t = t + table[5, i] * v
        return (a, b, s, t)

    sums = lax.fori_loop(0, CHUNKS, step, (zero, zero, zero, zero))
    for at in range(4):
        vec_ref[at] = sums[at]
    vec_ref[4] = v_ref[0]
    vec_ref[5] = v_ref[span - 1]


def local_sums(table, velocity, weight):
    span, planes, width = velocity.shape
    return pl.pallas_call(
        sums_kernel,
        out_shape=jax.ShapeDtypeStruct((6, planes, width), F32),
        in_specs=in_smem(1) + in_vmem(2),
        out_specs=in_vmem(1)[0],
        compiler_params=vmem(8),
        cost_estimate=work(8 * velocity.size, 4 * velocity.size),
        name="local_sums",
    )(table, velocity, weight)


def slope_kernel(table, metric, v_hbm, order, out_hbm, v_ref, der, v_sem, out_sem):
    span, planes, width = v_ref.shape
    inner = span - 1
    rows = span // CHUNKS
    start_all(v_hbm, v_ref, v_sem)
    zero = jnp.zeros((planes, width), F32)
    top = jnp.where(lax.axis_index("gx") == 0, 1.0, 0.0).astype(F32)

    def forward(i, carry):
        v_low, v, slo = carry
        v_high = v_ref[i + 1]
        slo = table[0, i] * (v_high - v_low) + table[1, i] * slo
        if isinstance(i, int) and i == 0:
            slo = slo + (table[3, 0] * top) * v
        der[i] = slo
        return (v, v_high, slo)

    def down(c, carry):
        chunk_copy(v_hbm, v_ref, v_sem, c + 1).wait()
        for r in range(rows):
            carry = forward(c * rows + r, carry)
        return carry

    chunk_copy(v_hbm, v_ref, v_sem, 0).wait()
    carry = down(0, (zero, v_ref[0], zero))
    carry = lax.fori_loop(1, CHUNKS - 1, down, carry)
    for i in range(span - rows, inner):
        carry = forward(i, carry)

    def finish(i, slo, difference):
        scale = metric[i]
        return scale * slo + (scale * DIRECT) * difference

    def backward(i, slo, difference):
        slo = der[i] + table[2, i] * slo
        der[i] = finish(i, slo, difference)
        return slo

    def up(step, slo):
        c = CHUNKS - 1 - step
        for r in range(rows - 1, -1, -1):
            i = c * rows + r
            slo = backward(i, slo, v_ref[i + 1] - v_ref[i - 1])
        chunk_copy(der, out_hbm, out_sem, c).start()
        return slo

    der[inner] = finish(inner, zero, -v_ref[inner - 1])
    slo = zero
    for i in range(inner - 1, span - 1 - rows, -1):
        slo = backward(i, slo, v_ref[i + 1] - v_ref[i - 1])
    chunk_copy(der, out_hbm, out_sem, CHUNKS - 1).start()
    slo = lax.fori_loop(1, CHUNKS - 1, up, slo)
    for i in range(rows - 1, -1, -1):
        slo = backward(i, slo, v_ref[i + 1] - v_ref[i - 1] if i else v_ref[1])
    chunk_copy(der, out_hbm, out_sem, 0).start()
    for c in range(CHUNKS):
        chunk_copy(der, out_hbm, out_sem, c).wait()


def slope_solve(table, metric, velocity, order):
    return pl.pallas_call(
        slope_kernel,
        out_shape=pltpu.HBM(velocity.shape, F32),
        in_specs=in_smem(2) + in_hbm(1) + [pl.BlockSpec(memory_space=pl.ANY)],
        out_specs=in_hbm(1)[0],
        scratch_shapes=streamed(velocity.shape, 2) + [pltpu.SemaphoreType.DMA((CHUNKS,))] * 2,
        compiler_params=vmem(12),
        cost_estimate=work(12 * velocity.size, 12 * velocity.size),
        name="slope_solve",
    )(table, metric, velocity, order)


def viscous_kernel(
    v_hbm,
    line,
    before_ref,
    after_ref,
    cross_ref,
    order,
    out_hbm,
    kept,
    v_ref,
    upd,
    even,
    odd,
    v_sem,
    out_sem,
):
    span, planes, width = v_ref.shape
    inner = span - 1
    rows = span // CHUNKS
    start_all(v_hbm, v_ref, v_sem)
    lane = lane_of((planes, width))
    ahead = pltpu.roll(after_ref[...], width - 1, 1)
    even[...] = jnp.where(lax.rem(lane, 2) == 0, before_ref[...], ahead)
    odd[...] = jnp.where(lax.rem(lane, 2) == 1, before_ref[...], ahead)
    cross = jnp.broadcast_to(cross_ref[...], (planes, width))
    keep = 1.0 - 2.0 * cross
    zero = jnp.zeros((planes, width), F32)

    def forward(i, r, vis):
        v = v_ref[i]
        rim = (odd if r % 2 else even)[...]
        if r:
            rim = pltpu.roll(rim, width - r, 1)
        low = jnp.where(lane == 0, rim, pltpu.roll(v, 1, 1))
        high = jnp.where(lane == width - 1, rim, pltpu.roll(v, width - 1, 1))
        rhs = keep * v + cross * (low + high)
        vis = line[0, i] * rhs + line[1, i] * vis
        upd[i] = vis
        return vis

    def down(c, vis):
        chunk_copy(v_hbm, v_ref, v_sem, c).wait()
        for r in range(rows):
            vis = forward(c * rows + r, r, vis)
        even[...] = pltpu.roll(even[...], width - rows, 1)
        odd[...] = pltpu.roll(odd[...], width - rows, 1)
        return vis

    lax.fori_loop(0, CHUNKS, down, zero)

    base = (CHUNKS - KEPT) * rows

    def backward(i, vis):
        return upd[i] + line[2, i] * vis

    kept[inner - base] = zero
    vis = zero
    for i in range(inner - 1, span - 1 - rows, -1):
        vis = backward(i, vis)
        kept[i - base] = vis

    def keep_chunk(step, vis):
        for r in range(rows - 1, -1, -1):
            i = (CHUNKS - 1 - step) * rows + r
            vis = backward(i, vis)
            kept[i - base] = vis
        return vis

    vis = lax.fori_loop(1, KEPT, keep_chunk, vis)
    for c in range(CHUNKS - KEPT - 1, -1, -1):
        for r in range(rows - 1, -1, -1):
            i = c * rows + r
            vis = backward(i, vis)
            upd[i] = vis
        row_copy(upd, out_hbm, out_sem, c, rows).start()
    for c in range(CHUNKS - KEPT):
        row_copy(upd, out_hbm, out_sem, c, rows).wait()


def viscous_solve(velocity, line, before, after, cross, order):
    span, planes, width = velocity.shape
    kept = KEPT * (span // CHUNKS)
    return pl.pallas_call(
        viscous_kernel,
        out_shape=(
            pltpu.HBM((span - kept, planes, width), F32),
            pltpu.VMEM((kept, planes, width), F32),
        ),
        in_specs=in_hbm(1) + in_smem(1) + in_vmem(3) + [pl.BlockSpec(memory_space=pl.ANY)],
        out_specs=tuple(in_hbm(1) + in_vmem(1)),
        scratch_shapes=streamed(velocity.shape, 2)
        + [pltpu.VMEM((planes, width), F32)] * 2
        + [pltpu.SemaphoreType.DMA((CHUNKS,))] * 2,
        compiler_params=vmem(12),
        cost_estimate=work(12 * velocity.size, 12 * velocity.size),
        name="viscous_solve",
    )(velocity, line, before, after, cross, order)


def wall_normal(value, before, after, cross):
    shape = value.shape
    lane = lane_of(shape)
    low = jnp.where(lane == 0, before, pltpu.roll(value, 1, 1))
    high = jnp.where(lane == shape[1] - 1, after, pltpu.roll(value, shape[1] - 1, 1))
    return (1.0 - 2.0 * cross) * value + cross * (low + high)


def pack_kernel(vec_ref, row_ref, before_ref, after_ref, cross_ref, out_ref, token):
    blocks = out_ref.shape[0]
    part = vec_ref.shape[1] // blocks
    cross = cross_ref[...]
    vectors = []
    for at in range(2):
        weights = row_ref[at, 0:1, :]
        before = jnp.sum(before_ref[...] * weights, axis=1, keepdims=True)
        after = jnp.sum(after_ref[...] * weights, axis=1, keepdims=True)
        vectors.append(wall_normal(vec_ref[at], before, after, cross))
    vectors += [vec_ref[at] for at in range(2, 6)]
    for at, value in enumerate(vectors):
        for m in range(blocks):
            out_ref[m, at] = value[part * m : part * (m + 1), :]
    token[...] = jnp.zeros(token.shape, F32)


def pack(vec, row, before, after, cross, blocks):
    _, planes, width = vec.shape
    part = planes // blocks
    return pl.pallas_call(
        pack_kernel,
        out_shape=(jax.ShapeDtypeStruct((blocks, 6, part, width), F32), TOKEN),
        compiler_params=vmem(8),
        name="pack_sums",
    )(vec, row, before, after, cross)


def reduced_kernel(red, weights, coef_ref, in_ref, order, out_ref, token):
    blocks, _, part, width = in_ref.shape
    slope_after, slope_before = (weights["after"], weights["before"])

    def piece(k, at):
        return in_ref[k, at]

    zero = jnp.zeros((part, width), F32)
    vis, slo = (zero, zero)
    vis_all, slo_all = ([], [])
    for k in range(blocks):
        vis_rhs = piece(k, 0)
        slo_rhs = piece(k, 2)
        if k < blocks - 1:
            vis_rhs = vis_rhs + piece(k + 1, 1)
            slo_rhs = slo_rhs + piece(k + 1, 3) + slope_after * piece(k, 5)
        else:
            slo_rhs = slo_rhs + weights["last_end"] * piece(k, 5)
        if k > 0:
            slo_rhs = slo_rhs + slope_before * piece(k - 1, 5)
        else:
            slo_rhs = slo_rhs + weights["first_end"] * piece(k, 4)
        vis = coef_ref[0, k : k + 1, :] * vis_rhs + coef_ref[1, k : k + 1, :] * vis
        slo = red[k][0] * slo_rhs + red[k][1] * slo
        vis_all.append(vis)
        slo_all.append(slo)
    vis, slo = (zero, zero)
    for k in range(blocks - 1, -1, -1):
        vis = vis_all[k] + coef_ref[2, k : k + 1, :] * vis
        slo = slo_all[k] + red[k][2] * slo
        out_ref[k, 1] = vis
        out_ref[k, 3] = slo
        if k < blocks - 1:
            out_ref[k + 1, 0] = vis
            out_ref[k + 1, 2] = slo + (BODY / ALPHA) * piece(k, 5)
        else:
            out_ref[0, 0] = zero
            out_ref[0, 2] = zero
        out_ref[k, 4] = piece(k - 1, 5) if k > 0 else zero
        out_ref[k, 5] = piece(k + 1, 4) if k < blocks - 1 else zero
    token[...] = jnp.zeros(token.shape, F32)


def reduced_solve(coef, arrived, order, red, weights):
    return pl.pallas_call(
        functools.partial(reduced_kernel, red, weights),
        out_shape=(jax.ShapeDtypeStruct(arrived.shape, F32), TOKEN),
        in_specs=in_vmem(2) + in_hbm(1),
        out_specs=tuple(in_vmem(2)),
        compiler_params=vmem(8),
        name="reduced_solve",
    )(coef, arrived, order)


def final_kernel(
    table,
    metric,
    der_in,
    upd_in,
    kept,
    edge_ref,
    spike,
    der_hbm,
    upd_hbm,
    der,
    upd,
    edges,
    der_from,
    upd_from,
    der_to,
    upd_to,
):
    span, planes, width = der.shape
    blocks = edge_ref.shape[0]
    part = planes // blocks
    rows = span // CHUNKS
    far = CHUNKS - KEPT
    for c in range(CHUNKS - 1, -1, -1):
        row_copy(der_in, der, der_from, c, rows).start()
    for c in range(far - 1, -1, -1):
        row_copy(upd_in, upd, upd_from, c, rows).start()
    for at in range(6):
        for m in range(blocks):
            edges[at, part * m : part * (m + 1), :] = edge_ref[m, at]
    vis_low, vis_high, slo_low, slo_high = (edges[at] for at in range(4))

    def viscous_rows(c, source, base):
        for r in range(rows):
            i = c * rows + r
            low = spike[0, i] * vis_low
            high = spike[1, i] * vis_high
            upd[i] = source[i - base] + low + high
        row_copy(upd, upd_hbm, upd_to, c, rows).start()

    def slope_rows(c):
        row_copy(der_in, der, der_from, c, rows).wait()
        for r in range(rows):
            i = c * rows + r
            scale = metric[i]
            der[i] = der[i] + (scale * table[6, i]) * slo_low + (scale * table[7, i]) * slo_high
        if isinstance(c, int) and c == 0:
            der[0] = der[0] - (metric[0] * DIRECT) * edges[4]
        if isinstance(c, int) and c == CHUNKS - 1:
            der[span - 1] = der[span - 1] + (metric[span - 1] * DIRECT) * edges[5]
        row_copy(der, der_hbm, der_to, c, rows).start()

    def near_viscous(step, carry):
        viscous_rows(CHUNKS - 1 - step, kept, far * rows)
        return carry

    def near_slope(step, carry):
        slope_rows(CHUNKS - 1 - step)
        return carry

    lax.fori_loop(0, KEPT, near_viscous, 0)
    slope_rows(CHUNKS - 1)
    lax.fori_loop(1, KEPT, near_slope, 0)
    for c in range(far - 1, -1, -1):
        row_copy(upd_in, upd, upd_from, c, rows).wait()
        viscous_rows(c, upd, 0)
        slope_rows(c)
    for c in range(CHUNKS):
        row_copy(der, der_hbm, der_to, c, rows).wait()
        row_copy(upd, upd_hbm, upd_to, c, rows).wait()


def final_solve(table, metric, der, upd, kept, edge, spike):
    span, planes, width = der.shape
    result = jax.ShapeDtypeStruct(der.shape, F32)
    return pl.pallas_call(
        final_kernel,
        out_shape=(result, result),
        in_specs=in_smem(2) + in_hbm(2) + in_vmem(2) + in_smem(1),
        out_specs=tuple(in_hbm(2)),
        scratch_shapes=streamed(der.shape, 2)
        + [pltpu.VMEM((6, planes, width), F32)]
        + [pltpu.SemaphoreType.DMA((CHUNKS,))] * 4,
        compiler_params=vmem(12),
        name="final_solve",
    )(table, metric, der, upd, kept, edge, spike)


def body(velocity, metric, lower_coupling, upper_coupling, cross_diffusion):
    span, planes, width = velocity.shape
    blocks = lax.axis_size("gx")
    walls = lax.axis_size("gy")
    rows, red, weights = slope_constants(blocks, span)
    table = jnp.asarray(rows)
    cross = cross_diffusion.reshape(1, width)
    field = pltpu.with_memory_space_constraint(velocity, pltpu.HBM)
    lower = lower_coupling.reshape(blocks, span)
    upper = upper_coupling.reshape(blocks, span)
    near, first, last = rim_columns(field)
    up = [(j, j + 1) for j in range(walls - 1)]
    down = [(j + 1, j) for j in range(walls - 1)]
    before = lax.ppermute(last, "gy", up)
    after = lax.ppermute(first, "gy", down)
    line, weight, spike, row, coef = block_terms(lower, upper)
    vec = local_sums(table, near, weight)
    packed, token = pack(vec, row, before, after, cross, blocks)
    arrived = lax.all_to_all(packed, "gx", 0, 0, tiled=True)
    der = slope_solve(table, metric, field, token)
    der = pltpu.with_memory_space_constraint(der, pltpu.HBM)
    solved, token = reduced_solve(coef, arrived, der, red, weights)
    edge = lax.all_to_all(solved, "gx", 0, 0, tiled=True)
    upd, kept = viscous_solve(field, line, before, after, cross, token)
    upd = pltpu.with_memory_space_constraint(upd, pltpu.HBM)
    return final_solve(table, metric, der, upd, kept, edge, spike)


def solution(mesh):
    return jax.shard_map(
        body,
        mesh=mesh,
        in_specs=(P("gx", None, "gy"), P("gx"), P(), P(), P("gy")),
        out_specs=(P("gx", None, "gy"), P("gx", None, "gy")),
        check_vma=False,
    )
```
